32 devices in a mesh: dp: 8 (over y, x, core), fsdp: 4 (over z).
Axes of the slice: x: 2, y: 2, z: 4, core: 2. Of those that a mesh axis runs over, the one named last changes fastest.
Arguments:
- grads: bfloat16 [8, 1024, 2048], P('dp', None, 'fsdp'), may hold values from -0.44 to 0.44
- stats: float32 [8, 4, 512, 512], P('dp', 'fsdp'), may hold values from -0.08 to 2, as said below
- left_root: bfloat16 [1024, 2048], P(None, 'fsdp'), may hold values from -0.02 to 1, as said below
- right_root: bfloat16 [1024, 2048], P(None, 'fsdp'), may hold values from -1.25 to 1.25, as said below
- owners: int32 [4, 2], replicated, may hold values from 0 to 7, as said below
Outputs:
- update: bfloat16 [1024, 2048], P(None, 'fsdp')
- new_stats: float32 [8, 4, 512, 512], P('dp', 'fsdp')
- new_root: bfloat16 [1024, 2048], P(None, 'fsdp')
The draws below stay inside these ranges and needn't reach their ends.
Inputs may be any that keep to these rules, and one draw needn't show every extreme that they name: `stats`: symmetric in each slot. `left_root`: symmetric in each block. `right_root`: symmetric in each block. `owners`: the 2 entries of each row are distinct.
All inputs are finite; a program needn't handle non-finite values.
Results may differ from the reference program's by a relative error of at most 0.033.
Values may be sent and summed in bfloat16 or wider, within the bound.
A program may use at most 64 MiB of HBM per device.

```python
import jax
import jax.numpy as jnp
from jax import lax

BLOCK = 512
BLOCK_ROWS = 2
ROWS = 1024
COLS = 2048
N_DP = 8
N_FSDP = 4


def root_draw(key, low, high):
    noise_key = jax.random.fold_in(key, 21)
    diag_key = jax.random.fold_in(key, 22)
    noise = jnp.clip(jax.random.normal(noise_key, (BLOCK_ROWS, BLOCK, N_FSDP, BLOCK)), -6.0, 6.0)
    symmetric = 0.5 * (noise + jnp.transpose(noise, (0, 3, 2, 1)))
    diagonal = jnp.exp(jax.random.uniform(diag_key, (BLOCK_ROWS, BLOCK, N_FSDP), minval=jnp.log(low), maxval=jnp.log(high)))
    identity = jnp.eye(BLOCK, dtype=jnp.float32)[None, :, None, :]
    values = 0.003 * symmetric * (1.0 - identity) + identity * diagonal[..., None]
    return values.reshape(ROWS, COLS).astype(jnp.bfloat16)


def draw_grads(key, part):
    own_key = jax.random.fold_in(key, 1)
    row_key = jax.random.fold_in(key, 3)
    col_key = jax.random.fold_in(key, 4)
    noise = jnp.clip(jax.random.normal(own_key, (N_DP, ROWS, COLS)), -6.0, 6.0)
    row_scale = jnp.exp(jax.random.uniform(row_key, (ROWS,), minval=0.0, maxval=jnp.log(10.0)))
    col_scale = jnp.exp(jax.random.uniform(col_key, (COLS,), minval=0.0, maxval=jnp.log(10.0)))
    ramp = 1.0 + 2.0 * jnp.arange(COLS, dtype=jnp.float32) / (COLS - 1)
    values = 0.0002 * noise * row_scale[None, :, None] * (col_scale * ramp)[None, None, :]
    return values.astype(jnp.bfloat16)


def draw_stats(key, part):
    noise_key = jax.random.fold_in(key, 31)
    diag_key = jax.random.fold_in(key, 32)
    noise = jnp.clip(jax.random.normal(noise_key, (N_DP, N_FSDP, BLOCK, BLOCK)), -6.0, 6.0)
    symmetric = 0.5 * (noise + jnp.swapaxes(noise, 2, 3))
    diagonal = jnp.exp(jax.random.uniform(diag_key, (N_DP, N_FSDP, BLOCK), minval=0.0, maxval=jnp.log(2.0)))
    identity = jnp.eye(BLOCK, dtype=jnp.float32)
    values = 0.012 * symmetric * (1.0 - identity) + identity * diagonal[..., None]
    return values.astype(jnp.float32)


def draw_left_root(key, part):
    return root_draw(jax.random.fold_in(key, 41), 0.84, 1.0)


def draw_right_root(key, part):
    return root_draw(jax.random.fold_in(key, 51), 0.6, 1.2)


def one_permutation(row_key):
    return jax.random.permutation(row_key, N_DP)


def draw_owners(key, part):
    row_keys = jax.random.split(jax.random.fold_in(key, 61), N_FSDP)
    orders = jax.vmap(one_permutation)(row_keys).astype(jnp.int32)
    highest = N_DP - 1
    first_row = orders[0]
    first_row = jnp.where(first_row == highest, first_row[0], first_row).at[0].set(highest)
    second_row = orders[1]
    second_row = jnp.where(second_row == 0, second_row[0], second_row).at[0].set(0)
    orders = orders.at[0].set(first_row).at[1].set(second_row)
    return orders[:, :BLOCK_ROWS].astype(jnp.int32)


def setup_inputs(seed: int = 0) -> dict:
    key_of = jax.random.split(jax.random.key(seed), 6)
    grads = draw_grads(jax.random.fold_in(key_of[5], 71), 0)
    stats = draw_stats(jax.random.fold_in(key_of[5], 71), 0)
    left_root = draw_left_root(jax.random.fold_in(key_of[5], 71), 0)
    right_root = draw_right_root(jax.random.fold_in(key_of[5], 71), 0)
    owners = draw_owners(jax.random.fold_in(key_of[5], 71), 0)
    return dict(grads=grads, stats=stats, left_root=left_root, right_root=right_root, owners=owners)


BETA = 0.95
EPSILON = 1e-06

def precise(left_arg, right_arg):
    return jnp.dot(left_arg, right_arg, preferred_element_type=jnp.float32, precision=lax.Precision.HIGHEST)

def as_blocks(matrix):
    return matrix.reshape(BLOCK_ROWS, BLOCK, N_FSDP, BLOCK).transpose(2, 0, 1, 3).reshape(N_FSDP * BLOCK_ROWS, BLOCK, BLOCK)

def from_blocks(pieces):
    return pieces.reshape(N_FSDP, BLOCK_ROWS, BLOCK, BLOCK).transpose(1, 2, 0, 3).reshape(ROWS, COLS)

def per_block(block_items):
    grad_block, left_block, right_block, old_stats = block_items
    fresh_stats = BETA * old_stats + (1.0 - BETA) * jnp.einsum('ik,jk->ij', grad_block.astype(jnp.float32), grad_block.astype(jnp.float32))
    left_product = jnp.dot(left_block, grad_block, preferred_element_type=jnp.float32).astype(jnp.bfloat16)
    raw_update = jnp.dot(left_product, right_block, preferred_element_type=jnp.float32)
    start_root = left_block.astype(jnp.float32)
    square = precise(start_root, start_root)
    middle = precise(precise(square, fresh_stats), square)
    identity = jnp.eye(BLOCK, dtype=jnp.float32)
    refreshed = precise(start_root, (5.0 * identity - middle) * 0.25).astype(jnp.bfloat16)
    return (fresh_stats, raw_update.astype(jnp.bfloat16), jnp.sum(raw_update * raw_update), refreshed)

def reference(grads, stats, left_root, right_root, owners):
    total_grad = lax.optimization_barrier(jnp.sum(grads.astype(jnp.float32), axis=0))
    summed = total_grad.astype(jnp.bfloat16)
    columns = jnp.arange(N_FSDP, dtype=jnp.int32)[:, None]
    old_stats = stats[owners, columns].reshape(N_FSDP * BLOCK_ROWS, BLOCK, BLOCK)
    fresh_stats, rounded, squares, refreshed = lax.map(per_block, (as_blocks(summed), as_blocks(left_root), as_blocks(right_root), old_stats))
    rms_scale = lax.rsqrt(jnp.sum(squares) / (ROWS * COLS) + EPSILON)
    widened = lax.optimization_barrier(rounded).astype(jnp.float32)
    update = from_blocks((widened * rms_scale).astype(jnp.bfloat16))
    new_stats = jnp.zeros_like(stats).at[owners, columns].set(fresh_stats.reshape(N_FSDP, BLOCK_ROWS, BLOCK, BLOCK))
    new_root = from_blocks(refreshed)
    return (update, new_stats, new_root)
```

```python
import functools

import jax
import jax.numpy as jnp
from jax import lax
from jax.experimental import pallas as pl
from jax.experimental.pallas import tpu as pltpu
from jax.sharding import PartitionSpec as P

BETA = 0.95
EPSILON = 1e-06
MESH = pl.DeviceIdType.MESH
F32 = jnp.float32
BF16 = jnp.bfloat16


def mm(a, b):
    return jnp.dot(a, b, preferred_element_type=F32)


def mm_t(a, b):
    return lax.dot_general(a, b, (((1,), (1,)), ((), ())), preferred_element_type=F32)


class Stream:
    def __init__(self, me, order, block, source, kept, base, recv, part, whole, sems):
        self.order, self.block, self.n = order, block, len(order)
        self.source, self.kept, self.base = source, kept, base
        self.recv, self.part, self.whole = recv, part, whole
        self.rs_send, self.rs_recv, self.ag_send, self.ag_recv = sems
        self.bit = [(me // (1 << b)) % 2 for b in order]
        self.peer = [me + (1 - 2 * v) * (1 << b) for v, b in zip(self.bit, order)]
        self.half = [block >> (j + 1) for j in range(self.n)]
        self.at = [block - (block >> j) for j in range(self.n)]
        self.low = []
        low = 0
        for j in range(self.n):
            low = low + self.bit[j] * self.half[j]
            self.low.append(low)
        self.pending = []

    def rows(self, start, size):
        return pl.ds(pl.multiple_of(start, 16), size)

    def copy(self, src, dst, send, recv, peer):
        move = pltpu.make_async_remote_copy(
            src_ref=src,
            dst_ref=dst,
            send_sem=send,
            recv_sem=recv,
            device_id={"dp": peer},
            device_id_type=MESH,
        )
        move.start()
        self.pending.append(move)
        return move

    def start_sum(self, j):
        half = self.half[j]
        away = (1 - self.bit[j]) * half
        if j == 0:
            src = self.source.at[self.rows(self.base + away, half)]
        else:
            src = self.part.at[self.rows(self.at[j - 1] + away, half)]
        self.move = self.copy(
            src,
            self.recv.at[pl.ds(self.at[j], half)],
            self.rs_send.at[j],
            self.rs_recv.at[j],
            self.peer[j],
        )

    def added(self, j, offset, size):
        near = self.bit[j] * self.half[j] + offset
        if j == 0:
            mine = self.kept[self.rows(self.base + near, size), :]
        else:
            mine = self.part[self.rows(self.at[j - 1] + near, size), :]
        other = self.recv[self.rows(self.at[j] + offset, size), :]
        return (mine.astype(F32) + other.astype(F32)).astype(BF16)

    def end_sum(self, j):
        self.move.wait_recv()
        if j == self.n - 1:
            self.whole[self.rows(self.low[j], self.half[j]), :] = self.added(j, 0, self.half[j])
            self.start_spread(j)
            return
        quarter = self.half[j + 1]
        v = self.bit[j + 1]
        self.part[self.rows(self.at[j] + (1 - v) * quarter, quarter), :] = self.added(
            j, (1 - v) * quarter, quarter
        )
        self.start_sum(j + 1)
        self.part[self.rows(self.at[j] + v * quarter, quarter), :] = self.added(
            j, v * quarter, quarter
        )

    def start_spread(self, j):
        here = self.whole.at[self.rows(self.low[j], self.half[j])]
        self.move = self.copy(here, here, self.ag_send.at[j], self.ag_recv.at[j], self.peer[j])

    def end_spread(self, j):
        self.move.wait_recv()
        if j > 0:
            self.start_spread(j - 1)

    def finish(self):
        for move in self.pending:
            move.wait_send()


def kernel(
    n_dp, n_f, entries, owners, grads, stats, left, right, update, new_stats, new_root,
    v_grads, v_stats, v_left, v_right, masked, recv, part, whole, square_ref, rounded, outer_ref,
    slots, local_sem, rs_send, rs_recv, ag_send, ag_recv, z_send, z_recv,
):
    me = lax.axis_index("dp")
    col = lax.axis_index("fsdp")
    block = v_stats.shape[0]
    blocks = v_left.shape[0] // block
    bits = n_dp.bit_length() - 1

    loads = []
    for i, (src, dst) in enumerate(
        ((grads, v_grads), (stats, v_stats), (left, v_left), (right, v_right))
    ):
        load = pltpu.make_async_copy(src, dst, local_sem.at[i])
        load.start()
        loads.append(load)

    barrier = pltpu.get_barrier_semaphore()
    for b in range(bits):
        v = (me // (1 << b)) % 2
        pl.semaphore_signal(
            barrier, inc=1, device_id={"dp": me + (1 - 2 * v) * (1 << b)}, device_id_type=MESH
        )
    for o in range(1, n_f):
        pl.semaphore_signal(
            barrier, inc=1, device_id={"fsdp": lax.rem(col + o, n_f)}, device_id_type=MESH
        )
    pl.semaphore_wait(barrier, bits + n_f - 1)

    forward = list(range(bits))
    turned = [0] + forward[:0:-1]
    streams = []
    for k in range(2 * blocks):
        i = k % blocks
        of_grads = k < blocks
        streams.append(
            Stream(
                me, forward if i % 2 == 0 else turned, block,
                grads if of_grads else masked.at[i], v_grads if of_grads else masked.at[i],
                i * block if of_grads else 0,
                recv.at[k], part.at[k], whole.at[k],
                (rs_send.at[k], rs_recv.at[k], ag_send.at[k], ag_recv.at[k]),
            )
        )
    of_g, of_s = streams[:blocks], streams[blocks:]

    for s in of_g:
        s.start_sum(0)
    owns = [jnp.where(owners[col, i] == me, 1.0, 0.0).astype(F32) for i in range(blocks)]
    loads[1].wait()
    for i, s in enumerate(of_s):
        masked[i, :, :] = (v_stats[...] * owns[i]).astype(BF16)
        s.start_sum(0)
    loads[0].wait()
    for s in of_g:
        s.end_sum(0)
    for s in of_s:
        s.end_sum(0)
    loads[2].wait()
    for i in range(blocks):
        x = v_left[pl.ds(i * block, block), :]
        square_ref[i, :, :] = mm(x, x).astype(BF16)
    for j in range(1, bits):
        for s in streams:
            s.end_sum(j)
    for j in range(bits - 1, 0, -1):
        for s in of_g:
            s.end_spread(j)
        if j > 1:
            for s in of_s:
                s.end_spread(j)
    loads[3].wait()
    squares = jnp.zeros((8, 128), F32)
    for i, s in enumerate(of_g):
        s.end_spread(0)
        rows = pl.ds(i * block, block)
        product = mm(v_left[rows, :], whole[i, :, :]).astype(BF16)
        raw = mm(product, v_right[rows, :])
        rounded[rows, :] = raw.astype(BF16)
        power = jnp.sum((raw * raw).reshape(block // 8, 8, block), axis=0)
        for c in range(0, block, 128):
            squares = squares + power[:, c : c + 128]
    slots[pl.ds(col, 1), :, :] = squares[None]
    z_moves = []
    for o in range(1, n_f):
        move = pltpu.make_async_remote_copy(
            src_ref=slots.at[col],
            dst_ref=slots.at[col],
            send_sem=z_send.at[o - 1],
            recv_sem=z_recv.at[o - 1],
            device_id={"fsdp": lax.rem(col + o, n_f)},
            device_id_type=MESH,
        )
        move.start()
        z_moves.append(move)
    if bits > 1:
        for s in of_s:
            s.end_spread(1)
    for i in range(blocks):
        g = whole[i, :, :]
        outer_ref[i, :, :] = (1.0 - BETA) * mm_t(g, g)
    mine = BETA * v_stats[...] * sum(owns[1:], owns[0])
    for i in range(blocks):
        mine = mine + owns[i] * outer_ref[i, :, :]
    new_stats[...] = mine
    for i, s in enumerate(of_s):
        s.end_spread(0)
        x = v_left[pl.ds(i * block, block), :]
        q = square_ref[i, :, :]
        fresh = BETA * whole[blocks + i, :, :].astype(F32) + outer_ref[i, :, :]
        half_way = mm(q, fresh.astype(BF16)).astype(BF16)
        middle = mm(half_way, q).astype(BF16)
        new_root[pl.ds(i * block, block), :] = (
            1.25 * x.astype(F32) - 0.25 * mm(x, middle)
        ).astype(BF16)
    for move in z_moves:
        move.wait_recv()
    total = slots[0]
    for c in range(1, n_f):
        total = total + slots[c]
    total = jnp.sum(jnp.sum(total, axis=1, keepdims=True), axis=0, keepdims=True)
    scale = lax.rsqrt(total / entries + EPSILON)
    update[...] = (rounded[...].astype(F32) * scale).astype(BF16)
    for s in streams:
        s.finish()
    for move in z_moves:
        move.wait_send()


def solution(mesh):
    n_dp, n_f = mesh.shape["dp"], mesh.shape["fsdp"]
    bits = n_dp.bit_length() - 1

    def local(grads, stats, left, right, owners):
        block = stats.shape[-1]
        rows = left.shape[0]
        blocks = rows // block
        hbm = pl.BlockSpec(memory_space=pl.ANY)
        vmem = pl.BlockSpec(memory_space=pltpu.VMEM)
        dma = pltpu.SemaphoreType.DMA
        update, new_stats, new_root = pl.pallas_call(
            functools.partial(kernel, n_dp, n_f, rows * block * n_f),
            out_shape=(
                jax.ShapeDtypeStruct((rows, block), BF16),
                jax.ShapeDtypeStruct((block, block), F32),
                jax.ShapeDtypeStruct((rows, block), BF16),
            ),
            in_specs=[pl.BlockSpec(memory_space=pltpu.SMEM), hbm, hbm, hbm, hbm],
            out_specs=(vmem, vmem, vmem),
            scratch_shapes=[
                pltpu.VMEM((rows, block), BF16),
                pltpu.VMEM((block, block), F32),
                pltpu.VMEM((rows, block), BF16),
                pltpu.VMEM((rows, block), BF16),
                pltpu.VMEM((blocks, block, block), BF16),
                pltpu.VMEM((2 * blocks, block, block), BF16),
                pltpu.VMEM((2 * blocks, block, block), BF16),
                pltpu.VMEM((2 * blocks, block, block), BF16),
                pltpu.VMEM((blocks, block, block), BF16),
                pltpu.VMEM((rows, block), BF16),
                pltpu.VMEM((blocks, block, block), F32),
                pltpu.VMEM((n_f, 8, 128), F32),
                dma((4,)),
                dma((2 * blocks, bits)),
                dma((2 * blocks, bits)),
                dma((2 * blocks, bits)),
                dma((2 * blocks, bits)),
                dma((max(n_f - 1, 1),)),
                dma((max(n_f - 1, 1),)),
            ],
            compiler_params=pltpu.CompilerParams(
                collective_id=0, has_side_effects=True, vmem_limit_bytes=48 << 20
            ),
        )(owners, grads[0], stats[0, 0], left, right)
        return update, new_stats[None, None], new_root

    in_specs = (
        P("dp", None, "fsdp"),
        P("dp", "fsdp", None, None),
        P(None, "fsdp"),
        P(None, "fsdp"),
        P(),
    )
    out_specs = (P(None, "fsdp"), P("dp", "fsdp", None, None), P(None, "fsdp"))
    return jax.shard_map(local, mesh=mesh, in_specs=in_specs, out_specs=out_specs, check_vma=False)
```

```python
import functools

import jax
import jax.numpy as jnp
from jax import lax
from jax.experimental import pallas as pl
from jax.experimental.pallas import tpu as pltpu
from jax.sharding import PartitionSpec as P

BETA = 0.95
EPSILON = 1e-06
MESH = pl.DeviceIdType.MESH
F32 = jnp.float32
BF16 = jnp.bfloat16


def mm(a, b):
    return jnp.dot(a, b, preferred_element_type=F32)


def mm_t(a, b):
    return lax.dot_general(a, b, (((1,), (1,)), ((), ())), preferred_element_type=F32)


class Stream:
    def __init__(self, me, order, block, source, kept, base, recv, part, whole, sems):
        self.order, self.block, self.n = order, block, len(order)
        self.source, self.kept, self.base = source, kept, base
        self.recv, self.part, self.whole = recv, part, whole
        self.rs_send, self.rs_recv, self.ag_send, self.ag_recv = sems
        self.bit = [(me // (1 << b)) % 2 for b in order]
        self.peer = [me + (1 - 2 * v) * (1 << b) for v, b in zip(self.bit, order)]
        self.half = [block >> (j + 1) for j in range(self.n)]
        self.at = [block - (block >> j) for j in range(self.n)]
        self.low = []
        low = 0
        for j in range(self.n):
            low = low + self.bit[j] * self.half[j]
            self.low.append(low)
        self.pending = []

    def rows(self, start, size):
        return pl.ds(pl.multiple_of(start, 16), size)

    def copy(self, src, dst, send, recv, peer):
        move = pltpu.make_async_remote_copy(
            src_ref=src,
            dst_ref=dst,
            send_sem=send,
            recv_sem=recv,
            device_id={"dp": peer},
            device_id_type=MESH,
        )
        move.start()
        self.pending.append(move)
        return move

    def start_sum(self, j):
        half = self.half[j]
        away = (1 - self.bit[j]) * half
        if j == 0:
            src = self.source.at[self.rows(self.base + away, half)]
        else:
            src = self.part.at[self.rows(self.at[j - 1] + away, half)]
        self.move = self.copy(
            src,
            self.recv.at[pl.ds(self.at[j], half)],
            self.rs_send.at[j],
            self.rs_recv.at[j],
            self.peer[j],
        )

    def added(self, j, offset, size):
        near = self.bit[j] * self.half[j] + offset
        if j == 0:
            mine = self.kept[self.rows(self.base + near, size), :]
        else:
            mine = self.part[self.rows(self.at[j - 1] + near, size), :]
        other = self.recv[self.rows(self.at[j] + offset, size), :]
        return (mine.astype(F32) + other.astype(F32)).astype(BF16)

    def end_sum(self, j):
        self.move.wait_recv()
        if j == self.n - 1:
            self.whole[self.rows(self.low[j], self.half[j]), :] = self.added(j, 0, self.half[j])
            self.start_spread(j)
            return
        quarter = self.half[j + 1]
        v = self.bit[j + 1]
        self.part[self.rows(self.at[j] + (1 - v) * quarter, quarter), :] = self.added(
            j, (1 - v) * quarter, quarter
        )
        self.start_sum(j + 1)
        self.part[self.rows(self.at[j] + v * quarter, quarter), :] = self.added(
            j, v * quarter, quarter
        )

    def start_spread(self, j):
        here = self.whole.at[self.rows(self.low[j], self.half[j])]
        self.move = self.copy(here, here, self.ag_send.at[j], self.ag_recv.at[j], self.peer[j])

    def end_spread(self, j):
        self.move.wait_recv()
        if j > 0:
            self.start_spread(j - 1)

    def finish(self):
        for move in self.pending:
            move.wait_send()


def tile_list(count, upper):
    return [(r, c) for r in range(count) for c in range(r if upper else 0, count)]


def kernel(
    n_dp, n_f, entries, tiles, upper, owners_hbm, grads, stats, left, right,
    update, new_stats, new_root,
    owners, v_grads, v_stats, v_left, v_right, masked, recv_g, part_g, whole_g,
    recv_a, part_a, whole_a, full, square_ref, rounded, base_ref,
    slots, local_sem, rs_send, rs_recv, ag_send, ag_recv, z_send, z_recv,
):
    me = lax.axis_index("dp")
    col = lax.axis_index("fsdp")
    block = v_stats.shape[0]
    blocks = v_left.shape[0] // block
    bits = n_dp.bit_length() - 1

    loads = []
    for i, (src, dst) in enumerate(
        (
            (owners_hbm, owners), (stats.at[0, 0], v_stats), (left, v_left),
            (grads.at[0], v_grads), (right, v_right),
        )
    ):
        load = pltpu.make_async_copy(src, dst, local_sem.at[i])
        load.start()
        loads.append(load)

    barrier = pltpu.get_barrier_semaphore()
    for b in range(bits):
        v = (me // (1 << b)) % 2
        pl.semaphore_signal(
            barrier, inc=1, device_id={"dp": me + (1 - 2 * v) * (1 << b)}, device_id_type=MESH
        )
    for o in range(1, n_f):
        pl.semaphore_signal(
            barrier, inc=1, device_id={"fsdp": lax.rem(col + o, n_f)}, device_id_type=MESH
        )
    pl.semaphore_wait(barrier, bits + n_f - 1)

    forward = list(range(bits))
    turned = [0] + forward[:0:-1]
    of_g, of_a = [], []
    for i in range(blocks):
        order = forward if i % 2 == 0 else turned
        k = blocks + i
        of_g.append(
            Stream(
                me, order, block, grads.at[0], v_grads, i * block,
                recv_g.at[i], part_g.at[i], whole_g.at[i],
                (rs_send.at[i], rs_recv.at[i], ag_send.at[i], ag_recv.at[i]),
            )
        )
        of_a.append(
            Stream(
                me, order, masked.shape[1], masked.at[i], masked.at[i], 0,
                recv_a.at[i], part_a.at[i], whole_a.at[i],
                (rs_send.at[k], rs_recv.at[k], ag_send.at[k], ag_recv.at[k]),
            )
        )
    streams = of_g + of_a

    for s in of_g:
        s.start_sum(0)
    for load in loads[:3]:
        load.wait()
    owns = [jnp.where(owners[i, col] == me, 1.0, 0.0).astype(F32) for i in range(blocks)]
    own_x = jnp.zeros((block, block), F32)
    for i in range(blocks):
        own_x = own_x + owns[i] * v_left[pl.ds(i * block, block), :].astype(F32)
    own_x = own_x.astype(BF16)
    own_q = mm(own_x, own_x).astype(BF16)
    own_a = mm(mm(own_q, v_stats[...].astype(BF16)).astype(BF16), own_q)
    for i, s in enumerate(of_a):
        mine = (own_a * owns[i]).astype(BF16)
        for k, (r, c) in enumerate(tiles):
            masked[i, pl.ds(k * 128, 128), :] = mine[
                r * 128 : (r + 1) * 128, c * 128 : (c + 1) * 128
            ]
        s.start_sum(0)
    loads[3].wait()
    for s in streams:
        s.end_sum(0)
    for i in range(blocks):
        x = v_left[pl.ds(i * block, block), :]
        square_ref[i, :, :] = mm(x, x).astype(BF16)
    for j in range(1, bits):
        for s in streams:
            s.end_sum(j)
    for j in range(bits - 1, 0, -1):
        for s in of_g:
            s.end_spread(j)
        if j > 1:
            for s in of_a:
                s.end_spread(j)
    loads[4].wait()
    squares = jnp.zeros((8, 128), F32)
    for i, s in enumerate(of_g):
        s.end_spread(0)
        rows = pl.ds(i * block, block)
        product = mm(v_left[rows, :], whole_g[i, :, :]).astype(BF16)
        raw = mm(product, v_right[rows, :])
        rounded[rows, :] = raw.astype(BF16)
        power = jnp.sum((raw * raw).reshape(block // 8, 8, block), axis=0)
        for c in range(0, block, 128):
            squares = squares + power[:, c : c + 128]
    slots[pl.ds(col, 1), :, :] = squares[None]
    z_moves = []
    for o in range(1, n_f):
        move = pltpu.make_async_remote_copy(
            src_ref=slots.at[col],
            dst_ref=slots.at[col],
            send_sem=z_send.at[o - 1],
            recv_sem=z_recv.at[o - 1],
            device_id={"fsdp": lax.rem(col + o, n_f)},
            device_id_type=MESH,
        )
        move.start()
        z_moves.append(move)
    if bits > 1:
        for s in of_a:
            s.end_spread(1)
    outer = jnp.zeros((block, block), F32)
    for i in range(blocks):
        g = whole_g[i, :, :]
        x = v_left[pl.ds(i * block, block), :]
        h = mm(square_ref[i, :, :], g).astype(BF16)
        extra = (((1.0 - BETA) * 0.25) * mm_t(h, h)).astype(BF16)
        base_ref[i, :, :] = 1.25 * x.astype(F32) - mm(x, extra)
        outer = outer + (owns[i] * (1.0 - BETA)) * mm_t(g, g)
    new_stats[...] = (BETA * sum(owns[1:], owns[0])) * v_stats[...] + outer
    for move in z_moves:
        move.wait_recv()
    total = slots[0]
    for c in range(1, n_f):
        total = total + slots[c]
    total = jnp.sum(jnp.sum(total, axis=1, keepdims=True), axis=0, keepdims=True)
    scale = lax.rsqrt(total / entries + EPSILON)
    update[...] = (rounded[...].astype(F32) * scale).astype(BF16)
    for i, s in enumerate(of_a):
        s.end_spread(0)
        for k, (r, c) in enumerate(tiles):
            tile = whole_a[i, pl.ds(k * 128, 128), :]
            full[i, pl.ds(r * 128, 128), pl.ds(c * 128, 128)] = tile
            if upper and r != c:
                full[i, pl.ds(c * 128, 128), pl.ds(r * 128, 128)] = tile.T
        rows = pl.ds(i * block, block)
        new_root[rows, :] = (
            base_ref[i, :, :] - (BETA * 0.25) * mm(v_left[rows, :], full[i, :, :])
        ).astype(BF16)
    for s in streams:
        s.finish()
    for move in z_moves:
        move.wait_send()


def write_out(*refs):
    sources, targets, sems = refs[:3], refs[3:6], refs[6]
    moves = [
        pltpu.make_async_copy(src, dst, sems.at[i])
        for i, (src, dst) in enumerate(zip(sources, targets))
    ]
    for move in moves:
        move.start()
    for move in moves:
        move.wait()


def solution(mesh):
    n_dp, n_f = mesh.shape["dp"], mesh.shape["fsdp"]
    bits = n_dp.bit_length() - 1

    def local(grads, stats, left, right, owners):
        block = stats.shape[-1]
        rows = left.shape[0]
        blocks = rows // block
        count = block // 128
        upper = (len(tile_list(count, True)) * 128) % (16 * n_dp) == 0
        tiles = tile_list(count, upper)
        size = len(tiles) * 128
        hbm = pl.BlockSpec(memory_space=pl.ANY)
        vmem = pl.BlockSpec(memory_space=pltpu.VMEM)
        dma = pltpu.SemaphoreType.DMA
        shapes = (
            jax.ShapeDtypeStruct((rows, block), BF16),
            jax.ShapeDtypeStruct((block, block), F32),
            jax.ShapeDtypeStruct((rows, block), BF16),
        )
        results = pl.pallas_call(
            functools.partial(kernel, n_dp, n_f, rows * block * n_f, tiles, upper),
            out_shape=shapes,
            in_specs=[pl.BlockSpec(memory_space=pltpu.HBM)] * 5,
            out_specs=(vmem, vmem, vmem),
            scratch_shapes=[
                pltpu.SMEM((blocks, n_f), jnp.int32),
                pltpu.VMEM((rows, block), BF16),
                pltpu.VMEM((block, block), F32),
                pltpu.VMEM((rows, block), BF16),
                pltpu.VMEM((rows, block), BF16),
                pltpu.VMEM((blocks, size, 128), BF16),
                pltpu.VMEM((blocks, block, block), BF16),
                pltpu.VMEM((blocks, block, block), BF16),
                pltpu.VMEM((blocks, block, block), BF16),
                pltpu.VMEM((blocks, size, 128), BF16),
                pltpu.VMEM((blocks, size, 128), BF16),
                pltpu.VMEM((blocks, size, 128), BF16),
                pltpu.VMEM((blocks, block, block), BF16),
                pltpu.VMEM((blocks, block, block), BF16),
                pltpu.VMEM((rows, block), BF16),
                pltpu.VMEM((blocks, block, block), F32),
                pltpu.VMEM((n_f, 8, 128), F32),
                dma((5,)),
                dma((2 * blocks, bits)),
                dma((2 * blocks, bits)),
                dma((2 * blocks, bits)),
                dma((2 * blocks, bits)),
                dma((max(n_f - 1, 1),)),
                dma((max(n_f - 1, 1),)),
            ],
            compiler_params=pltpu.CompilerParams(
                collective_id=0, has_side_effects=True, vmem_limit_bytes=50 << 20
            ),
        )(owners.T, grads, stats, left, right)
        update, new_stats, new_root = pl.pallas_call(
            write_out,
            out_shape=shapes,
            in_specs=[hbm] * 3,
            out_specs=(hbm, hbm, hbm),
            scratch_shapes=[dma((3,))],
            compiler_params=pltpu.CompilerParams(vmem_limit_bytes=50 << 20),
        )(*results)
        return update, new_stats[None, None], new_root

    in_specs = (
        P("dp", None, "fsdp"),
        P("dp", "fsdp", None, None),
        P(None, "fsdp"),
        P(None, "fsdp"),
        P(),
    )
    out_specs = (P(None, "fsdp"), P("dp", "fsdp", None, None), P(None, "fsdp"))
    return jax.shard_map(local, mesh=mesh, in_specs=in_specs, out_specs=out_specs, check_vma=False)
```

```python
import functools

import jax
import jax.numpy as jnp
from jax import lax
from jax.experimental import pallas as pl
from jax.experimental.pallas import tpu as pltpu
from jax.sharding import PartitionSpec as P

BETA = 0.95
EPSILON = 1e-06
MESH = pl.DeviceIdType.MESH
F32 = jnp.float32
BF16 = jnp.bfloat16


def mm(a, b):
    return jnp.dot(a, b, preferred_element_type=F32)


def mm_t(a, b):
    return lax.dot_general(a, b, (((1,), (1,)), ((), ())), preferred_element_type=F32)


class Stream:
    def __init__(self, me, order, size, source, kept, near, away, recv, part, whole, base, sems):
        self.order, self.size, self.n = order, size, len(order)
        self.source, self.kept, self.near, self.away = source, kept, near, away
        self.recv, self.part, self.whole = recv, part, whole
        self.rs_send, self.rs_recv, self.ag_send, self.ag_recv = sems
        self.bit = [(me // (1 << b)) % 2 for b in order]
        self.peer = [me + (1 - 2 * v) * (1 << b) for v, b in zip(self.bit, order)]
        self.half = [size >> j for j in range(self.n)]
        self.at = [0] + [2 * size - (size >> (j - 1)) for j in range(1, self.n)]
        self.low = [base]
        for j in range(1, self.n):
            self.low.append(self.low[-1] + self.bit[j] * self.half[j])
        self.pending = []

    def rows(self, start, size):
        return pl.ds(pl.multiple_of(start, 16), size)

    def copy(self, src, dst, send, recv, peer):
        move = pltpu.make_async_remote_copy(
            src_ref=src,
            dst_ref=dst,
            send_sem=send,
            recv_sem=recv,
            device_id={"dp": peer},
            device_id_type=MESH,
        )
        move.start()
        self.pending.append(move)
        return move

    def start_sum(self, j):
        half = self.half[j]
        if j == 0:
            src = self.source.at[self.rows(self.away, half)]
        else:
            src = self.part.at[self.rows(self.at[j - 1] + (1 - self.bit[j]) * half, half)]
        self.move = self.copy(
            src,
            self.recv.at[pl.ds(self.at[j], half)],
            self.rs_send.at[j],
            self.rs_recv.at[j],
            self.peer[j],
        )

    def added(self, j, offset, size):
        if j == 0:
            mine = self.kept[self.rows(self.near + offset, size), :]
        else:
            near = self.at[j - 1] + self.bit[j] * self.half[j]
            mine = self.part[self.rows(near + offset, size), :]
        other = self.recv[self.rows(self.at[j] + offset, size), :]
        return (mine.astype(F32) + other.astype(F32)).astype(BF16)

    def end_sum(self, j):
        self.move.wait_recv()
        if j == self.n - 1:
            self.whole[self.rows(self.low[j], self.half[j]), :] = self.added(j, 0, self.half[j])
            if j > 0:
                self.start_spread(j)
            return
        quarter = self.half[j + 1]
        v = self.bit[j + 1]
        self.part[self.rows(self.at[j] + (1 - v) * quarter, quarter), :] = self.added(
            j, (1 - v) * quarter, quarter
        )
        self.start_sum(j + 1)
        self.part[self.rows(self.at[j] + v * quarter, quarter), :] = self.added(
            j, v * quarter, quarter
        )

    def start_spread(self, j):
        here = self.whole.at[self.rows(self.low[j], self.half[j])]
        self.move = self.copy(here, here, self.ag_send.at[j], self.ag_recv.at[j], self.peer[j])

    def end_spread(self, j):
        self.move.wait_recv()
        if j > 1:
            self.start_spread(j - 1)

    def finish(self):
        for move in self.pending:
            move.wait_send()


def tile_list(count, upper):
    return [(r, c) for r in range(count) for c in range(r if upper else 0, count)]


def kernel(
    n_dp, n_f, entries, tiles, upper, owners_hbm, grads, stats, left, right,
    update, new_stats, new_root,
    owners, v_grads, v_stats, v_left, v_right, masked, recv_g, part_g, whole_g,
    recv_a, part_a, whole_a, full, rounded, extra,
    slots, local_sem, rs_send, rs_recv, ag_send, ag_recv, x_send, x_recv, z_send, z_recv,
):
    me = lax.axis_index("dp")
    col = lax.axis_index("fsdp")
    block = v_stats.shape[0]
    size = whole_a.shape[0]
    bits = n_dp.bit_length() - 1
    core = me % 2
    twin = me + 1 - 2 * core
    here = pl.ds(pl.multiple_of(core * block, block), block)

    loads = []
    for i, (src, dst) in enumerate(
        (
            (owners_hbm, owners), (stats.at[0, 0], v_stats), (left, v_left),
            (grads.at[0], v_grads), (right.at[here], v_right),
        )
    ):
        load = pltpu.make_async_copy(src, dst, local_sem.at[i])
        load.start()
        loads.append(load)

    partners = [{"dp": me + (1 - 2 * ((me // (1 << b)) % 2)) * (1 << b)} for b in range(bits)]
    others = []
    for o in range(1, n_f):
        others.append({"fsdp": lax.rem(col + o, n_f)})
        others.append({"dp": twin, "fsdp": lax.rem(col + o, n_f)})
    barrier = pltpu.get_barrier_semaphore()
    for device in partners + others:
        pl.semaphore_signal(barrier, inc=1, device_id=device, device_id_type=MESH)
    pl.semaphore_wait(barrier, len(partners) + len(others))
    others.append({"dp": twin})

    forward = list(range(bits))
    turned = [0] + forward[:0:-1]
    of_g, of_a = [], []
    for k in range(2):
        order = forward if k == 0 else turned
        share = block // 2
        of_g.append(
            Stream(
                me, order, share, grads.at[0], v_grads,
                core * block + k * share, (1 - core) * block + k * share,
                recv_g.at[k], part_g.at[k], whole_g, core * block + k * share,
                (rs_send.at[k], rs_recv.at[k], ag_send.at[k], ag_recv.at[k]),
            )
        )
        share = size // 2
        of_a.append(
            Stream(
                me, order, share, masked, masked,
                core * size + k * share, (1 - core) * size + k * share,
                recv_a.at[k], part_a.at[k], whole_a, k * share,
                (rs_send.at[2 + k], rs_recv.at[2 + k], ag_send.at[2 + k], ag_recv.at[2 + k]),
            )
        )
    streams = of_g + of_a
    swaps = []

    def swap(src, dst):
        move = pltpu.make_async_remote_copy(
            src_ref=src,
            dst_ref=dst,
            send_sem=x_send.at[len(swaps)],
            recv_sem=x_recv.at[len(swaps)],
            device_id={"dp": twin},
            device_id_type=MESH,
        )
        move.start()
        swaps.append(move)

    for s in of_g:
        s.start_sum(0)
    for load in loads[:3]:
        load.wait()
    owns = [jnp.where(owners[i, col] == me, 1.0, 0.0).astype(F32) for i in range(2)]

    def owned(ref):
        first = owns[0] * ref[pl.ds(0, block), :].astype(F32)
        return (first + owns[1] * ref[pl.ds(block, block), :].astype(F32)).astype(BF16)

    own_x = owned(v_left)
    own_q = mm(own_x, own_x).astype(BF16)
    own_t = mm(own_q, v_stats[...].astype(BF16)).astype(BF16)
    loads[3].wait()
    for s in of_g:
        s.end_sum(0)
    own_a = mm(own_t, own_q)
    for i in range(2):
        mine = (own_a * owns[i]).astype(BF16)
        for k, (r, c) in enumerate(tiles):
            masked[pl.ds(i * size + k * 128, 128), :] = mine[
                r * 128 : (r + 1) * 128, c * 128 : (c + 1) * 128
            ]
    for s in of_a:
        s.start_sum(0)
    x = v_left[here, :]
    q = mm(x, x).astype(BF16)
    for s in of_a:
        s.end_sum(0)
    for j in range(1, bits):
        for s in streams:
            s.end_sum(j)
    for j in range(bits - 1, 0, -1):
        for s in of_g:
            s.end_spread(j)
        if j > 1:
            for s in of_a:
                s.end_spread(j)
    swap(whole_g.at[here], whole_g.at[here])
    loads[4].wait()
    g = whole_g[here, :]
    raw = mm(mm(x, g).astype(BF16), v_right[...])
    rounded[here, :] = raw.astype(BF16)
    swap(rounded.at[here], rounded.at[here])
    power = jnp.sum((raw * raw).reshape(block // 8, 8, block), axis=0)
    squares = jnp.zeros((8, 128), F32)
    for c in range(0, block, 128):
        squares = squares + power[:, c : c + 128]
    slot = core * n_f + col
    slots[pl.ds(slot, 1), :, :] = squares[None]
    z_moves = []
    for i, device in enumerate(others):
        move = pltpu.make_async_remote_copy(
            src_ref=slots.at[slot],
            dst_ref=slots.at[slot],
            send_sem=z_send.at[i],
            recv_sem=z_recv.at[i],
            device_id=device,
            device_id_type=MESH,
        )
        move.start()
        z_moves.append(move)
    h = mm(q, g).astype(BF16)
    extra[...] = (1.0 - BETA) * mm_t(h, h)
    swaps[0].wait_recv()
    own_g = owned(whole_g)
    has = owns[0] + owns[1]
    new_stats[...] = (BETA * has) * v_stats[...] + (1.0 - BETA) * mm_t(own_g, own_g)
    for move in z_moves:
        move.wait_recv()
    total = slots[0]
    for c in range(1, 2 * n_f):
        total = total + slots[c]
    total = jnp.sum(jnp.sum(total, axis=1, keepdims=True), axis=0, keepdims=True)
    scale = lax.rsqrt(total / entries + EPSILON)
    swaps[1].wait_recv()
    update[...] = (rounded[...].astype(F32) * scale).astype(BF16)
    if bits > 1:
        for s in of_a:
            s.end_spread(1)
    for k, (r, c) in enumerate(tiles):
        down, along = pl.ds(r * 128, 128), pl.ds(c * 128, 128)
        middle = BETA * whole_a[pl.ds(k * 128, 128), :].astype(F32) + extra[down, along]
        middle = middle.astype(BF16)
        full[down, along] = middle
        if upper and r != c:
            full[along, down] = middle.T
    middle = full[...]
    share = block // 2
    for k in range(2):
        rows = pl.ds(pl.multiple_of(core * block + k * share, share), share)
        some = v_left[rows, :]
        new_root[rows, :] = (1.25 * some.astype(F32) - 0.25 * mm(some, middle)).astype(BF16)
        swap(new_root.at[rows], new_root.at[rows])
    for move in swaps[2:]:
        move.wait_recv()
    for s in streams:
        s.finish()
    for move in swaps + z_moves:
        move.wait_send()


def write_out(*refs):
    sources, targets, sems = refs[:3], refs[3:6], refs[6]
    moves = [
        pltpu.make_async_copy(src, dst, sems.at[i])
        for i, (src, dst) in enumerate(zip(sources, targets))
    ]
    for move in moves:
        move.start()
    for move in moves:
        move.wait()


def solution(mesh):
    n_dp, n_f = mesh.shape["dp"], mesh.shape["fsdp"]
    bits = n_dp.bit_length() - 1

    def local(grads, stats, left, right, owners):
        block = stats.shape[-1]
        rows = left.shape[0]
        count = block // 128
        upper = (len(tile_list(count, True)) * 128) % (16 * n_dp) == 0
        tiles = tile_list(count, upper)
        size = len(tiles) * 128
        hbm = pl.BlockSpec(memory_space=pl.ANY)
        vmem = pl.BlockSpec(memory_space=pltpu.VMEM)
        dma = pltpu.SemaphoreType.DMA
        shapes = (
            jax.ShapeDtypeStruct((rows, block), BF16),
            jax.ShapeDtypeStruct((block, block), F32),
            jax.ShapeDtypeStruct((rows, block), BF16),
        )
        results = pl.pallas_call(
            functools.partial(kernel, n_dp, n_f, rows * block * n_f, tiles, upper),
            out_shape=shapes,
            in_specs=[pl.BlockSpec(memory_space=pltpu.HBM)] * 5,
            out_specs=(vmem, vmem, vmem),
            scratch_shapes=[
                pltpu.SMEM((2, n_f), jnp.int32),
                pltpu.VMEM((rows, block), BF16),
                pltpu.VMEM((block, block), F32),
                pltpu.VMEM((rows, block), BF16),
                pltpu.VMEM((block, block), BF16),
                pltpu.VMEM((2 * size, 128), BF16),
                pltpu.VMEM((2, block, block), BF16),
                pltpu.VMEM((2, block, block), BF16),
                pltpu.VMEM((rows, block), BF16),
                pltpu.VMEM((2, size, 128), BF16),
                pltpu.VMEM((2, size, 128), BF16),
                pltpu.VMEM((size, 128), BF16),
                pltpu.VMEM((block, block), BF16),
                pltpu.VMEM((rows, block), BF16),
                pltpu.VMEM((block, block), F32),
                pltpu.VMEM((2 * n_f, 8, 128), F32),
                dma((5,)),
                dma((4, bits)),
                dma((4, bits)),
                dma((4, bits)),
                dma((4, bits)),
                dma((4,)),
                dma((4,)),
                dma((2 * n_f - 1,)),
                dma((2 * n_f - 1,)),
            ],
            compiler_params=pltpu.CompilerParams(
                collective_id=0, has_side_effects=True, vmem_limit_bytes=50 << 20
            ),
        )(owners.T, grads, stats, left, right)
        update, new_stats, new_root = pl.pallas_call(
            write_out,
            out_shape=shapes,
            in_specs=[hbm] * 3,
            out_specs=(hbm, hbm, hbm),
            scratch_shapes=[dma((3,))],
            compiler_params=pltpu.CompilerParams(vmem_limit_bytes=50 << 20),
        )(*results)
        return update, new_stats[None, None], new_root

    in_specs = (
        P("dp", None, "fsdp"),
        P("dp", "fsdp", None, None),
        P(None, "fsdp"),
        P(None, "fsdp"),
        P(),
    )
    out_specs = (P(None, "fsdp"), P("dp", "fsdp", None, None), P(None, "fsdp"))
    return jax.shard_map(local, mesh=mesh, in_specs=in_specs, out_specs=out_specs, check_vma=False)
```

```python
import functools

import jax
import jax.numpy as jnp
from jax import lax
from jax.experimental import pallas as pl
from jax.experimental.pallas import tpu as pltpu
from jax.sharding import PartitionSpec as P

BETA = 0.95
EPSILON = 1e-06
MESH = pl.DeviceIdType.MESH
F32 = jnp.float32
BF16 = jnp.bfloat16


def mm(a, b):
    return jnp.dot(a, b, preferred_element_type=F32)


def mm_t(a, b):
    return lax.dot_general(a, b, (((1,), (1,)), ((), ())), preferred_element_type=F32)


class Stream:
    def __init__(self, me, order, size, source, kept, near, away, recv, part, whole, base, sems):
        self.order, self.size, self.n = order, size, len(order)
        self.source, self.kept, self.near, self.away = source, kept, near, away
        self.recv, self.part, self.whole = recv, part, whole
        self.rs_send, self.rs_recv, self.ag_send, self.ag_recv = sems
        self.bit = [(me // (1 << b)) % 2 for b in order]
        self.peer = [me + (1 - 2 * v) * (1 << b) for v, b in zip(self.bit, order)]
        self.half = [size >> min(j, max(self.n - 2, 0)) for j in range(self.n)]
        self.at = [0] + [2 * size - (size >> (j - 1)) for j in range(1, self.n)]
        self.low = [base]
        for j in range(1, self.n - 1):
            self.low.append(self.low[-1] + self.bit[j] * self.half[j])
        self.pending = []

    def rows(self, start, size):
        return pl.ds(pl.multiple_of(start, 16), size)

    def copy(self, src, dst, send, recv, peer):
        move = pltpu.make_async_remote_copy(
            src_ref=src,
            dst_ref=dst,
            send_sem=send,
            recv_sem=recv,
            device_id={"dp": peer},
            device_id_type=MESH,
        )
        move.start()
        self.pending.append(move)
        return move

    def skip(self, j, v):
        return 0 if j == self.n - 1 else v * self.half[j]

    def start_sum(self, j):
        half = self.half[j]
        if j == 0:
            src = self.source.at[self.rows(self.away, half)]
        else:
            src = self.part.at[self.rows(self.at[j - 1] + self.skip(j, 1 - self.bit[j]), half)]
        self.move = self.copy(
            src,
            self.recv.at[pl.ds(self.at[j], half)],
            self.rs_send.at[j],
            self.rs_recv.at[j],
            self.peer[j],
        )

    def added(self, j, offset, size):
        if j == 0:
            mine = self.kept[self.rows(self.near + offset, size), :]
        else:
            near = self.at[j - 1] + self.skip(j, self.bit[j])
            mine = self.part[self.rows(near + offset, size), :]
        other = self.recv[self.rows(self.at[j] + offset, size), :]
        return (mine.astype(F32) + other.astype(F32)).astype(BF16)

    def end_sum(self, j):
        self.move.wait_recv()
        if j == self.n - 1:
            self.whole[self.rows(self.low[-1], self.half[j]), :] = self.added(j, 0, self.half[j])
            if j > 1:
                self.start_spread(j - 1)
            return
        if j == self.n - 2:
            self.part[self.rows(self.at[j], self.half[j]), :] = self.added(j, 0, self.half[j])
            self.start_sum(j + 1)
            return
        quarter = self.half[j + 1]
        v = self.bit[j + 1]
        self.part[self.rows(self.at[j] + (1 - v) * quarter, quarter), :] = self.added(
            j, (1 - v) * quarter, quarter
        )
        self.start_sum(j + 1)
        self.part[self.rows(self.at[j] + v * quarter, quarter), :] = self.added(
            j, v * quarter, quarter
        )

    def start_spread(self, j):
        here = self.whole.at[self.rows(self.low[j], self.half[j])]
        self.move = self.copy(here, here, self.ag_send.at[j], self.ag_recv.at[j], self.peer[j])

    def end_spread(self, j):
        self.move.wait_recv()
        if j > 1:
            self.start_spread(j - 1)

    def finish(self):
        for move in self.pending:
            move.wait_send()


def tile_list(count, upper):
    return [(r, c) for r in range(count) for c in range(r if upper else 0, count)]


def kernel(
    n_dp, n_f, entries, tiles, upper, owners_hbm, grads, stats, left, right,
    update, new_stats, new_root,
    owners, v_grads, v_stats, v_left, v_right, masked, recv_g, part_g, whole_g,
    recv_a, part_a, whole_a, full, rounded, extra,
    slots, local_sem, rs_send, rs_recv, ag_send, ag_recv, x_send, x_recv, z_send, z_recv,
):
    me = lax.axis_index("dp")
    col = lax.axis_index("fsdp")
    block = v_stats.shape[0]
    size = whole_a.shape[0]
    bits = n_dp.bit_length() - 1
    core = me % 2
    twin = me + 1 - 2 * core
    here = pl.ds(pl.multiple_of(core * block, block), block)

    loads = []
    for i, (src, dst) in enumerate(
        (
            (owners_hbm, owners), (stats.at[0, 0], v_stats), (left, v_left),
            (grads.at[0], v_grads), (right.at[here], v_right),
        )
    ):
        load = pltpu.make_async_copy(src, dst, local_sem.at[i])
        load.start()
        loads.append(load)

    partners = [{"dp": me + (1 - 2 * ((me // (1 << b)) % 2)) * (1 << b)} for b in range(bits)]
    others = []
    for o in range(1, n_f):
        others.append({"fsdp": lax.rem(col + o, n_f)})
        others.append({"dp": twin, "fsdp": lax.rem(col + o, n_f)})
    barrier = pltpu.get_barrier_semaphore()
    for device in partners + others:
        pl.semaphore_signal(barrier, inc=1, device_id=device, device_id_type=MESH)
    pl.semaphore_wait(barrier, len(partners) + len(others))
    others.append({"dp": twin})

    forward = list(range(bits))
    turned = [0] + forward[:0:-1]
    of_g, of_a = [], []
    for k in range(2):
        order = forward if k == 0 else turned
        share = block // 2
        of_g.append(
            Stream(
                me, order, share, grads.at[0], v_grads,
                core * block + k * share, (1 - core) * block + k * share,
                recv_g.at[k], part_g.at[k], whole_g, core * block + k * share,
                (rs_send.at[k], rs_recv.at[k], ag_send.at[k], ag_recv.at[k]),
            )
        )
        share = size // 2
        of_a.append(
            Stream(
                me, order, share, masked, masked,
                core * size + k * share, (1 - core) * size + k * share,
                recv_a.at[k], part_a.at[k], whole_a, k * share,
                (rs_send.at[2 + k], rs_recv.at[2 + k], ag_send.at[2 + k], ag_recv.at[2 + k]),
            )
        )
    streams = of_g + of_a
    swaps = []

    def swap(src, dst):
        move = pltpu.make_async_remote_copy(
            src_ref=src,
            dst_ref=dst,
            send_sem=x_send.at[len(swaps)],
            recv_sem=x_recv.at[len(swaps)],
            device_id={"dp": twin},
            device_id_type=MESH,
        )
        move.start()
        swaps.append(move)

    for s in of_g:
        s.start_sum(0)
    for load in loads[:3]:
        load.wait()
    owns = [jnp.where(owners[i, col] == me, 1.0, 0.0).astype(F32) for i in range(2)]

    def owned(ref):
        first = owns[0] * ref[pl.ds(0, block), :].astype(F32)
        return (first + owns[1] * ref[pl.ds(block, block), :].astype(F32)).astype(BF16)

    own_x = owned(v_left)
    own_q = mm(own_x, own_x).astype(BF16)
    own_t = mm(own_q, v_stats[...].astype(BF16)).astype(BF16)
    loads[3].wait()
    for s in of_g:
        s.end_sum(0)
    own_a = mm(own_t, own_q)
    for i in range(2):
        mine = (own_a * owns[i]).astype(BF16)
        for k, (r, c) in enumerate(tiles):
            masked[pl.ds(i * size + k * 128, 128), :] = mine[
                r * 128 : (r + 1) * 128, c * 128 : (c + 1) * 128
            ]
    for s in of_a:
        s.start_sum(0)
    x = v_left[here, :]
    q = mm(x, x).astype(BF16)
    for s in of_a:
        s.end_sum(0)
    for j in range(1, bits):
        for s in streams:
            s.end_sum(j)
    for j in range(bits - 2, 0, -1):
        for s in of_g:
            s.end_spread(j)
        if j > 1:
            for s in of_a:
                s.end_spread(j)
    swap(whole_g.at[here], whole_g.at[here])
    loads[4].wait()
    g = whole_g[here, :]
    raw = mm(mm(x, g).astype(BF16), v_right[...])
    rounded[here, :] = raw.astype(BF16)
    swap(rounded.at[here], rounded.at[here])
    power = jnp.sum((raw * raw).reshape(block // 8, 8, block), axis=0)
    squares = jnp.zeros((8, 128), F32)
    for c in range(0, block, 128):
        squares = squares + power[:, c : c + 128]
    slot = core * n_f + col
    slots[pl.ds(slot, 1), :, :] = squares[None]
    z_moves = []
    for i, device in enumerate(others):
        move = pltpu.make_async_remote_copy(
            src_ref=slots.at[slot],
            dst_ref=slots.at[slot],
            send_sem=z_send.at[i],
            recv_sem=z_recv.at[i],
            device_id=device,
            device_id_type=MESH,
        )
        move.start()
        z_moves.append(move)
    h = mm(q, g).astype(BF16)
    extra[...] = (1.0 - BETA) * mm_t(h, h)
    if bits > 2:
        for s in of_a:
            s.end_spread(1)
    for k, (r, c) in enumerate(tiles):
        down, along = pl.ds(r * 128, 128), pl.ds(c * 128, 128)
        middle = BETA * whole_a[pl.ds(k * 128, 128), :].astype(F32) + extra[down, along]
        middle = middle.astype(BF16)
        full[down, along] = middle
        if upper and r != c:
            full[along, down] = middle.T
    middle = full[...]
    share = block // 4
    for k in range(4):
        rows = pl.ds(pl.multiple_of(core * block + k * share, share), share)
        some = v_left[rows, :]
        new_root[rows, :] = (1.25 * some.astype(F32) - 0.25 * mm(some, middle)).astype(BF16)
        swap(new_root.at[rows], new_root.at[rows])
    swaps[0].wait_recv()
    own_g = owned(whole_g)
    has = owns[0] + owns[1]
    new_stats[...] = (BETA * has) * v_stats[...] + (1.0 - BETA) * mm_t(own_g, own_g)
    for move in z_moves:
        move.wait_recv()
    total = slots[0]
    for c in range(1, 2 * n_f):
        total = total + slots[c]
    total = jnp.sum(jnp.sum(total, axis=1, keepdims=True), axis=0, keepdims=True)
    scale = lax.rsqrt(total / entries + EPSILON)
    swaps[1].wait_recv()
    update[...] = (rounded[...].astype(F32) * scale).astype(BF16)
    for move in swaps[2:]:
        move.wait_recv()
    for s in streams:
        s.finish()
    for move in swaps + z_moves:
        move.wait_send()


def write_out(*refs):
    sources, targets, sems = refs[:3], refs[3:6], refs[6]
    moves = [
        pltpu.make_async_copy(src, dst, sems.at[i])
        for i, (src, dst) in enumerate(zip(sources, targets))
    ]
    for move in moves:
        move.start()
    for move in moves:
        move.wait()


def solution(mesh):
    n_dp, n_f = mesh.shape["dp"], mesh.shape["fsdp"]
    bits = n_dp.bit_length() - 1

    def local(grads, stats, left, right, owners):
        block = stats.shape[-1]
        rows = left.shape[0]
        count = block // 128
        upper = (len(tile_list(count, True)) * 128) % (16 * n_dp) == 0
        tiles = tile_list(count, upper)
        size = len(tiles) * 128
        hbm = pl.BlockSpec(memory_space=pl.ANY)
        vmem = pl.BlockSpec(memory_space=pltpu.VMEM)
        dma = pltpu.SemaphoreType.DMA
        shapes = (
            jax.ShapeDtypeStruct((rows, block), BF16),
            jax.ShapeDtypeStruct((block, block), F32),
            jax.ShapeDtypeStruct((rows, block), BF16),
        )
        results = pl.pallas_call(
            functools.partial(kernel, n_dp, n_f, rows * block * n_f, tiles, upper),
            out_shape=shapes,
            in_specs=[pl.BlockSpec(memory_space=pltpu.HBM)] * 5,
            out_specs=(vmem, vmem, vmem),
            scratch_shapes=[
                pltpu.SMEM((2, n_f), jnp.int32),
                pltpu.VMEM((rows, block), BF16),
                pltpu.VMEM((block, block), F32),
                pltpu.VMEM((rows, block), BF16),
                pltpu.VMEM((block, block), BF16),
                pltpu.VMEM((2 * size, 128), BF16),
                pltpu.VMEM((2, block, block), BF16),
                pltpu.VMEM((2, block, block), BF16),
                pltpu.VMEM((rows, block), BF16),
                pltpu.VMEM((2, size, 128), BF16),
                pltpu.VMEM((2, size, 128), BF16),
                pltpu.VMEM((size, 128), BF16),
                pltpu.VMEM((block, block), BF16),
                pltpu.VMEM((rows, block), BF16),
                pltpu.VMEM((block, block), F32),
                pltpu.VMEM((2 * n_f, 8, 128), F32),
                dma((5,)),
                dma((4, bits)),
                dma((4, bits)),
                dma((4, bits)),
                dma((4, bits)),
                dma((6,)),
                dma((6,)),
                dma((2 * n_f - 1,)),
                dma((2 * n_f - 1,)),
            ],
            compiler_params=pltpu.CompilerParams(
                collective_id=0, has_side_effects=True, vmem_limit_bytes=50 << 20
            ),
        )(owners.T, grads, stats, left, right)
        update, new_stats, new_root = pl.pallas_call(
            write_out,
            out_shape=shapes,
            in_specs=[hbm] * 3,
            out_specs=(hbm, hbm, hbm),
            scratch_shapes=[dma((3,))],
            compiler_params=pltpu.CompilerParams(vmem_limit_bytes=50 << 20),
        )(*results)
        return update, new_stats[None, None], new_root

    in_specs = (
        P("dp", None, "fsdp"),
        P("dp", "fsdp", None, None),
        P(None, "fsdp"),
        P(None, "fsdp"),
        P(),
    )
    out_specs = (P(None, "fsdp"), P("dp", "fsdp", None, None), P(None, "fsdp"))
    return jax.shard_map(local, mesh=mesh, in_specs=in_specs, out_specs=out_specs, check_vma=False)
```

```python
import functools

import jax
import jax.numpy as jnp
from jax import lax
from jax.experimental import pallas as pl
from jax.experimental.pallas import tpu as pltpu
from jax.sharding import PartitionSpec as P

BETA = 0.95
EPSILON = 1e-06
MESH = pl.DeviceIdType.MESH
F32 = jnp.float32
BF16 = jnp.bfloat16


def mm(a, b):
    return jnp.dot(a, b, preferred_element_type=F32)


def mm_t(a, b):
    return lax.dot_general(a, b, (((1,), (1,)), ((), ())), preferred_element_type=F32)


class Stream:
    def __init__(self, me, order, size, source, kept, near, away, recv, part, whole, base, sems):
        self.order, self.size, self.n = order, size, len(order)
        self.source, self.kept, self.near, self.away = source, kept, near, away
        self.recv, self.part, self.whole = recv, part, whole
        self.rs_send, self.rs_recv, self.ag_send, self.ag_recv = sems
        self.bit = [(me // (1 << b)) % 2 for b in order]
        self.peer = [me + (1 - 2 * v) * (1 << b) for v, b in zip(self.bit, order)]
        self.half = [size >> min(j, max(self.n - 2, 0)) for j in range(self.n)]
        self.at = [0] + [2 * size - (size >> (j - 1)) for j in range(1, self.n)]
        self.low = [base]
        for j in range(1, self.n - 1):
            self.low.append(self.low[-1] + self.bit[j] * self.half[j])
        self.pending = []

    def rows(self, start, size):
        return pl.ds(pl.multiple_of(start, 16), size)

    def copy(self, src, dst, send, recv, peer):
        move = pltpu.make_async_remote_copy(
            src_ref=src,
            dst_ref=dst,
            send_sem=send,
            recv_sem=recv,
            device_id={"dp": peer},
            device_id_type=MESH,
        )
        move.start()
        self.pending.append(move)
        return move

    def skip(self, j, v):
        return 0 if j == self.n - 1 else v * self.half[j]

    def start_sum(self, j):
        half = self.half[j]
        if j == 0:
            src = self.source.at[self.rows(self.away, half)]
        else:
            src = self.part.at[self.rows(self.at[j - 1] + self.skip(j, 1 - self.bit[j]), half)]
        self.move = self.copy(
            src,
            self.recv.at[pl.ds(self.at[j], half)],
            self.rs_send.at[j],
            self.rs_recv.at[j],
            self.peer[j],
        )

    def added(self, j, offset, size):
        if j == 0:
            mine = self.kept[self.rows(self.near + offset, size), :]
        else:
            near = self.at[j - 1] + self.skip(j, self.bit[j])
            mine = self.part[self.rows(near + offset, size), :]
        other = self.recv[self.rows(self.at[j] + offset, size), :]
        return (mine.astype(F32) + other.astype(F32)).astype(BF16)

    def end_sum(self, j):
        self.move.wait_recv()
        if j == self.n - 1:
            self.whole[self.rows(self.low[-1], self.half[j]), :] = self.added(j, 0, self.half[j])
            if j > 1:
                self.start_spread(j - 1)
            return
        if j == self.n - 2:
            self.part[self.rows(self.at[j], self.half[j]), :] = self.added(j, 0, self.half[j])
            self.start_sum(j + 1)
            return
        quarter = self.half[j + 1]
        v = self.bit[j + 1]
        self.part[self.rows(self.at[j] + (1 - v) * quarter, quarter), :] = self.added(
            j, (1 - v) * quarter, quarter
        )
        self.start_sum(j + 1)
        self.part[self.rows(self.at[j] + v * quarter, quarter), :] = self.added(
            j, v * quarter, quarter
        )

    def start_spread(self, j):
        here = self.whole.at[self.rows(self.low[j], self.half[j])]
        self.move = self.copy(here, here, self.ag_send.at[j], self.ag_recv.at[j], self.peer[j])

    def end_spread(self, j):
        self.move.wait_recv()
        if j > 1:
            self.start_spread(j - 1)

    def finish(self):
        for move in self.pending:
            move.wait_send()


def tile_list(count, upper):
    return [(r, c) for r in range(count) for c in range(r if upper else 0, count)]


def kernel(
    n_dp, n_f, entries, tiles, upper, owners_hbm, grads, stats, left, right,
    update, new_stats, new_root,
    owners, v_grads, v_stats, v_left, v_right, masked, recv_g, part_g, whole_g,
    recv_a, part_a, whole_a, full, rounded, extra,
    slots, local_sem, rs_send, rs_recv, ag_send, ag_recv, x_send, x_recv, z_send, z_recv,
):
    me = lax.axis_index("dp")
    col = lax.axis_index("fsdp")
    block = v_stats.shape[0]
    size = whole_a.shape[0]
    bits = n_dp.bit_length() - 1
    core = me % 2
    twin = me + 1 - 2 * core
    here = pl.ds(pl.multiple_of(core * block, block), block)

    loads = []
    for i, (src, dst) in enumerate(
        (
            (owners_hbm, owners), (stats.at[0, 0], v_stats), (left, v_left),
            (grads.at[0], v_grads), (right.at[here], v_right),
        )
    ):
        load = pltpu.make_async_copy(src, dst, local_sem.at[i])
        load.start()
        loads.append(load)

    partners = [{"dp": me + (1 - 2 * ((me // (1 << b)) % 2)) * (1 << b)} for b in range(bits)]
    others = []
    for o in range(1, n_f):
        others.append({"fsdp": lax.rem(col + o, n_f)})
        others.append({"dp": twin, "fsdp": lax.rem(col + o, n_f)})
    barrier = pltpu.get_barrier_semaphore()
    for device in partners + others:
        pl.semaphore_signal(barrier, inc=1, device_id=device, device_id_type=MESH)
    pl.semaphore_wait(barrier, len(partners) + len(others))
    others.append({"dp": twin})

    forward = list(range(bits))
    turned = [0] + forward[:0:-1]
    of_g, of_a = [], []
    for k in range(recv_g.shape[0]):
        order = forward if k % 2 == 0 else turned
        share = block // recv_g.shape[0]
        of_g.append(
            Stream(
                me, order, share, grads.at[0], v_grads,
                core * block + k * share, (1 - core) * block + k * share,
                recv_g.at[k], part_g.at[k], whole_g, core * block + k * share,
                (rs_send.at[k], rs_recv.at[k], ag_send.at[k], ag_recv.at[k]),
            )
        )
    for k in range(2):
        order = forward if k == 0 else turned
        share = size // 2
        e = len(of_g) + k
        of_a.append(
            Stream(
                me, order, share, masked, masked,
                core * size + k * share, (1 - core) * size + k * share,
                recv_a.at[k], part_a.at[k], whole_a, k * share,
                (rs_send.at[e], rs_recv.at[e], ag_send.at[e], ag_recv.at[e]),
            )
        )
    streams = of_g + of_a
    swaps = []

    def swap(src, dst):
        move = pltpu.make_async_remote_copy(
            src_ref=src,
            dst_ref=dst,
            send_sem=x_send.at[len(swaps)],
            recv_sem=x_recv.at[len(swaps)],
            device_id={"dp": twin},
            device_id_type=MESH,
        )
        move.start()
        swaps.append(move)

    for s in of_g:
        s.start_sum(0)
    for load in loads[:3]:
        load.wait()
    owns = [jnp.where(owners[i, col] == me, 1.0, 0.0).astype(F32) for i in range(2)]

    def owned(ref):
        first = owns[0] * ref[pl.ds(0, block), :].astype(F32)
        return (first + owns[1] * ref[pl.ds(block, block), :].astype(F32)).astype(BF16)

    own_x = owned(v_left)
    own_q = mm(own_x, own_x).astype(BF16)
    own_t = mm(own_q, v_stats[...].astype(BF16)).astype(BF16)
    loads[3].wait()
    for s in of_g:
        s.end_sum(0)
    own_a = mm(own_t, own_q)
    for i in range(2):
        mine = (own_a * owns[i]).astype(BF16)
        for k, (r, c) in enumerate(tiles):
            masked[pl.ds(i * size + k * 128, 128), :] = mine[
                r * 128 : (r + 1) * 128, c * 128 : (c + 1) * 128
            ]
    for s in of_a:
        s.start_sum(0)
    x = v_left[here, :]
    q = mm(x, x).astype(BF16)
    for s in of_a:
        s.end_sum(0)
    for j in range(1, bits):
        for s in streams:
            s.end_sum(j)
    for j in range(bits - 2, 0, -1):
        for s in of_g:
            s.end_spread(j)
        if j > 1:
            for s in of_a:
                s.end_spread(j)
    swap(whole_g.at[here], whole_g.at[here])
    loads[4].wait()
    g = whole_g[here, :]
    raw = mm(mm(x, g).astype(BF16), v_right[...])
    rounded[here, :] = raw.astype(BF16)
    swap(rounded.at[here], rounded.at[here])
    power = jnp.sum((raw * raw).reshape(block // 8, 8, block), axis=0)
    squares = jnp.zeros((8, 128), F32)
    for c in range(0, block, 128):
        squares = squares + power[:, c : c + 128]
    slot = core * n_f + col
    slots[pl.ds(slot, 1), :, :] = squares[None]
    z_moves = []
    for i, device in enumerate(others):
        move = pltpu.make_async_remote_copy(
            src_ref=slots.at[slot],
            dst_ref=slots.at[slot],
            send_sem=z_send.at[i],
            recv_sem=z_recv.at[i],
            device_id=device,
            device_id_type=MESH,
        )
        move.start()
        z_moves.append(move)
    h = mm(q, g).astype(BF16)
    extra[...] = (1.0 - BETA) * mm_t(h, h)
    if bits > 2:
        for s in of_a:
            s.end_spread(1)
    for k, (r, c) in enumerate(tiles):
        down, along = pl.ds(r * 128, 128), pl.ds(c * 128, 128)
        middle = BETA * whole_a[pl.ds(k * 128, 128), :].astype(F32) + extra[down, along]
        middle = middle.astype(BF16)
        full[down, along] = middle
        if upper and r != c:
            full[along, down] = middle.T
    middle = full[...]
    share = block // 4
    for k in range(4):
        rows = pl.ds(pl.multiple_of(core * block + k * share, share), share)
        some = v_left[rows, :]
        new_root[rows, :] = (1.25 * some.astype(F32) - 0.25 * mm(some, middle)).astype(BF16)
        swap(new_root.at[rows], new_root.at[rows])
    swaps[0].wait_recv()
    own_g = owned(whole_g)
    has = owns[0] + owns[1]
    new_stats[...] = (BETA * has) * v_stats[...] + (1.0 - BETA) * mm_t(own_g, own_g)
    for move in z_moves:
        move.wait_recv()
    total = slots[0]
    for c in range(1, 2 * n_f):
        total = total + slots[c]
    total = jnp.sum(jnp.sum(total, axis=1, keepdims=True), axis=0, keepdims=True)
    scale = lax.rsqrt(total / entries + EPSILON)
    swaps[1].wait_recv()
    update[...] = (rounded[...].astype(F32) * scale).astype(BF16)
    for move in swaps[2:]:
        move.wait_recv()
    for s in streams:
        s.finish()
    for move in swaps + z_moves:
        move.wait_send()


def write_out(*refs):
    sources, targets, sems = refs[:3], refs[3:6], refs[6]
    pieces = sems.shape[1]
    moves = []
    for i, (src, dst) in enumerate(zip(sources, targets)):
        share = src.shape[0] // pieces
        for k in range(pieces):
            rows = pl.ds(k * share, share)
            moves.append(pltpu.make_async_copy(src.at[rows], dst.at[rows], sems.at[i, k]))
    for move in moves:
        move.start()
    for move in moves:
        move.wait()


def solution(mesh):
    n_dp, n_f = mesh.shape["dp"], mesh.shape["fsdp"]
    bits = n_dp.bit_length() - 1

    def local(grads, stats, left, right, owners):
        block = stats.shape[-1]
        rows = left.shape[0]
        count = block // 128
        upper = (len(tile_list(count, True)) * 128) % (16 * n_dp) == 0
        tiles = tile_list(count, upper)
        size = len(tiles) * 128
        parts = 4 if block % (32 * n_dp) == 0 else 2
        hbm = pl.BlockSpec(memory_space=pl.ANY)
        vmem = pl.BlockSpec(memory_space=pltpu.VMEM)
        dma = pltpu.SemaphoreType.DMA
        shapes = (
            jax.ShapeDtypeStruct((rows, block), BF16),
            jax.ShapeDtypeStruct((block, block), F32),
            jax.ShapeDtypeStruct((rows, block), BF16),
        )
        results = pl.pallas_call(
            functools.partial(kernel, n_dp, n_f, rows * block * n_f, tiles, upper),
            out_shape=shapes,
            in_specs=[pl.BlockSpec(memory_space=pltpu.HBM)] * 5,
            out_specs=(vmem, vmem, vmem),
            scratch_shapes=[
                pltpu.SMEM((2, n_f), jnp.int32),
                pltpu.VMEM((rows, block), BF16),
                pltpu.VMEM((block, block), F32),
                pltpu.VMEM((rows, block), BF16),
                pltpu.VMEM((block, block), BF16),
                pltpu.VMEM((2 * size, 128), BF16),
                pltpu.VMEM((parts, 2 * block // parts, block), BF16),
                pltpu.VMEM((parts, 2 * block // parts, block), BF16),
                pltpu.VMEM((rows, block), BF16),
                pltpu.VMEM((2, size, 128), BF16),
                pltpu.VMEM((2, size, 128), BF16),
                pltpu.VMEM((size, 128), BF16),
                pltpu.VMEM((block, block), BF16),
                pltpu.VMEM((rows, block), BF16),
                pltpu.VMEM((block, block), F32),
                pltpu.VMEM((2 * n_f, 8, 128), F32),
                dma((5,)),
                dma((parts + 2, bits)),
                dma((parts + 2, bits)),
                dma((parts + 2, bits)),
                dma((parts + 2, bits)),
                dma((6,)),
                dma((6,)),
                dma((2 * n_f - 1,)),
                dma((2 * n_f - 1,)),
            ],
            compiler_params=pltpu.CompilerParams(
                collective_id=0, has_side_effects=True, vmem_limit_bytes=50 << 20
            ),
        )(owners.T, grads, stats, left, right)
        update, new_stats, new_root = pl.pallas_call(
            write_out,
            out_shape=shapes,
            in_specs=[hbm] * 3,
            out_specs=(hbm, hbm, hbm),
            scratch_shapes=[dma((3, 4))],
            compiler_params=pltpu.CompilerParams(vmem_limit_bytes=50 << 20),
        )(*results)
        return update, new_stats[None, None], new_root

    in_specs = (
        P("dp", None, "fsdp"),
        P("dp", "fsdp", None, None),
        P(None, "fsdp"),
        P(None, "fsdp"),
        P(),
    )
    out_specs = (P(None, "fsdp"), P("dp", "fsdp", None, None), P(None, "fsdp"))
    return jax.shard_map(local, mesh=mesh, in_specs=in_specs, out_specs=out_specs, check_vma=False)
```

```python
import functools

import jax
import jax.numpy as jnp
from jax import lax
from jax.experimental import pallas as pl
from jax.experimental.pallas import tpu as pltpu
from jax.sharding import PartitionSpec as P

BETA = 0.95
EPSILON = 1e-06
MESH = pl.DeviceIdType.MESH
F32 = jnp.float32
BF16 = jnp.bfloat16


def mm(a, b):
    return jnp.dot(a, b, preferred_element_type=F32)


def mm_t(a, b):
    return lax.dot_general(a, b, (((1,), (1,)), ((), ())), preferred_element_type=F32)


class Stream:
    def __init__(self, me, order, size, source, kept, near, away, recv, part, whole, base, sems):
        self.order, self.size, self.n = order, size, len(order)
        self.source, self.kept, self.near, self.away = source, kept, near, away
        self.recv, self.part, self.whole = recv, part, whole
        self.rs_send, self.rs_recv, self.ag_send, self.ag_recv = sems
        self.bit = [(me // (1 << b)) % 2 for b in order]
        self.peer = [me + (1 - 2 * v) * (1 << b) for v, b in zip(self.bit, order)]
        self.half = [size >> min(j, max(self.n - 2, 0)) for j in range(self.n)]
        self.at = [0] + [2 * size - (size >> (j - 1)) for j in range(1, self.n)]
        self.low = [base]
        for j in range(1, self.n - 1):
            self.low.append(self.low[-1] + self.bit[j] * self.half[j])
        self.pending = []

    def rows(self, start, size):
        return pl.ds(pl.multiple_of(start, 16), size)

    def copy(self, src, dst, send, recv, peer):
        move = pltpu.make_async_remote_copy(
            src_ref=src,
            dst_ref=dst,
            send_sem=send,
            recv_sem=recv,
            device_id={"dp": peer},
            device_id_type=MESH,
        )
        move.start()
        self.pending.append(move)
        return move

    def skip(self, j, v):
        return 0 if j == self.n - 1 else v * self.half[j]

    def start_sum(self, j):
        half = self.half[j]
        if j == 0:
            src = self.source.at[self.rows(self.away, half)]
        else:
            src = self.part.at[self.rows(self.at[j - 1] + self.skip(j, 1 - self.bit[j]), half)]
        self.move = self.copy(
            src,
            self.recv.at[pl.ds(self.at[j], half)],
            self.rs_send.at[j],
            self.rs_recv.at[j],
            self.peer[j],
        )

    def added(self, j, offset, size):
        if j == 0:
            mine = self.kept[self.rows(self.near + offset, size), :]
        else:
            near = self.at[j - 1] + self.skip(j, self.bit[j])
            mine = self.part[self.rows(near + offset, size), :]
        other = self.recv[self.rows(self.at[j] + offset, size), :]
        return (mine.astype(F32) + other.astype(F32)).astype(BF16)

    def end_sum(self, j):
        self.move.wait_recv()
        if j == self.n - 1:
            self.whole[self.rows(self.low[-1], self.half[j]), :] = self.added(j, 0, self.half[j])
            if j > 1:
                self.start_spread(j - 1)
            return
        if j == self.n - 2:
            self.part[self.rows(self.at[j], self.half[j]), :] = self.added(j, 0, self.half[j])
            self.start_sum(j + 1)
            return
        quarter = self.half[j + 1]
        v = self.bit[j + 1]
        self.part[self.rows(self.at[j] + (1 - v) * quarter, quarter), :] = self.added(
            j, (1 - v) * quarter, quarter
        )
        self.start_sum(j + 1)
        self.part[self.rows(self.at[j] + v * quarter, quarter), :] = self.added(
            j, v * quarter, quarter
        )

    def start_spread(self, j):
        here = self.whole.at[self.rows(self.low[j], self.half[j])]
        self.move = self.copy(here, here, self.ag_send.at[j], self.ag_recv.at[j], self.peer[j])

    def end_spread(self, j):
        self.move.wait_recv()
        if j > 1:
            self.start_spread(j - 1)

    def finish(self):
        for move in self.pending:
            move.wait_send()


def tile_list(count, upper):
    return [(r, c) for r in range(count) for c in range(r if upper else 0, count)]


def kernel(
    n_dp, n_f, entries, tiles, upper, owners_hbm, grads, stats, left, right,
    update, new_stats, new_root,
    owners, v_grads, v_stats, v_left, v_right, masked, recv_g, part_g, whole_g,
    recv_a, part_a, whole_a, full, rounded, extra,
    slots, local_sem, rs_send, rs_recv, ag_send, ag_recv, x_send, x_recv, z_send, z_recv,
):
    me = lax.axis_index("dp")
    col = lax.axis_index("fsdp")
    block = v_stats.shape[0]
    size = whole_a.shape[0]
    bits = n_dp.bit_length() - 1
    core = me % 2
    twin = me + 1 - 2 * core
    here = pl.ds(pl.multiple_of(core * block, block), block)

    loads = []
    for i, (src, dst) in enumerate(
        (
            (owners_hbm, owners), (stats.at[0, 0], v_stats), (left, v_left),
            (grads.at[0, here], v_grads), (right.at[here], v_right),
        )
    ):
        load = pltpu.make_async_copy(src, dst, local_sem.at[i])
        load.start()
        loads.append(load)

    partners = [{"dp": me + (1 - 2 * ((me // (1 << b)) % 2)) * (1 << b)} for b in range(bits)]
    others = []
    for o in range(1, n_f):
        others.append({"fsdp": lax.rem(col + o, n_f)})
        others.append({"dp": twin, "fsdp": lax.rem(col + o, n_f)})
    barrier = pltpu.get_barrier_semaphore()
    for device in partners + others:
        pl.semaphore_signal(barrier, inc=1, device_id=device, device_id_type=MESH)
    pl.semaphore_wait(barrier, len(partners) + len(others))
    others.append({"dp": twin})

    forward = list(range(bits))
    turned = [0] + forward[:0:-1]
    of_g, of_a = [], []
    for k in range(recv_g.shape[0]):
        order = forward if k % 2 == 0 else turned
        share = block // recv_g.shape[0]
        of_g.append(
            Stream(
                me, order, share, grads.at[0], v_grads,
                k * share, (1 - core) * block + k * share,
                recv_g.at[k], part_g.at[k], whole_g, core * block + k * share,
                (rs_send.at[k], rs_recv.at[k], ag_send.at[k], ag_recv.at[k]),
            )
        )
    for k in range(recv_a.shape[0]):
        order = forward if k % 2 == 0 else turned
        share = size // recv_a.shape[0]
        e = len(of_g) + k
        of_a.append(
            Stream(
                me, order, share, masked, masked,
                core * size + k * share, (1 - core) * size + k * share,
                recv_a.at[k], part_a.at[k], whole_a, k * share,
                (rs_send.at[e], rs_recv.at[e], ag_send.at[e], ag_recv.at[e]),
            )
        )
    streams = of_g + of_a
    swaps = []

    def swap(src, dst):
        move = pltpu.make_async_remote_copy(
            src_ref=src,
            dst_ref=dst,
            send_sem=x_send.at[len(swaps)],
            recv_sem=x_recv.at[len(swaps)],
            device_id={"dp": twin},
            device_id_type=MESH,
        )
        move.start()
        swaps.append(move)

    for s in of_g:
        s.start_sum(0)
    for load in loads[:3]:
        load.wait()
    owns = [jnp.where(owners[i, col] == me, 1.0, 0.0).astype(F32) for i in range(2)]

    def owned(ref):
        first = owns[0] * ref[pl.ds(0, block), :].astype(F32)
        return (first + owns[1] * ref[pl.ds(block, block), :].astype(F32)).astype(BF16)

    own_x = owned(v_left)
    own_q = mm(own_x, own_x).astype(BF16)
    loads[3].wait()
    for s in of_g[:2]:
        s.end_sum(0)
    own_t = mm(own_q, v_stats[...].astype(BF16)).astype(BF16)
    for s in of_g[2:]:
        s.end_sum(0)
    own_a = mm(own_t, own_q)
    for i in range(2):
        mine = (own_a * owns[i]).astype(BF16)
        for k, (r, c) in enumerate(tiles):
            masked[pl.ds(i * size + k * 128, 128), :] = mine[
                r * 128 : (r + 1) * 128, c * 128 : (c + 1) * 128
            ]
    for s in of_a:
        s.start_sum(0)
    x = v_left[here, :]
    q = mm(x, x).astype(BF16)
    for s in of_a:
        s.end_sum(0)
    for j in range(1, bits):
        for s in streams:
            s.end_sum(j)
    for j in range(bits - 2, 0, -1):
        for s in of_g:
            s.end_spread(j)
        if j > 1:
            for s in of_a:
                s.end_spread(j)
    swap(whole_g.at[here], whole_g.at[here])
    loads[4].wait()
    g = whole_g[here, :]
    raw = mm(mm(x, g).astype(BF16), v_right[...])
    rounded[here, :] = raw.astype(BF16)
    swap(rounded.at[here], rounded.at[here])
    power = jnp.sum((raw * raw).reshape(block // 8, 8, block), axis=0)
    squares = jnp.zeros((8, 128), F32)
    for c in range(0, block, 128):
        squares = squares + power[:, c : c + 128]
    slot = core * n_f + col
    slots[pl.ds(slot, 1), :, :] = squares[None]
    z_moves = []
    for i, device in enumerate(others):
        move = pltpu.make_async_remote_copy(
            src_ref=slots.at[slot],
            dst_ref=slots.at[slot],
            send_sem=z_send.at[i],
            recv_sem=z_recv.at[i],
            device_id=device,
            device_id_type=MESH,
        )
        move.start()
        z_moves.append(move)
    h = mm(q, g).astype(BF16)
    extra[...] = (1.0 - BETA) * mm_t(h, h)
    done = 0
    for i, s in enumerate(of_a):
        if bits > 2:
            s.end_spread(1)
        ready = (i + 1) * s.size // 128
        for k in range(done, ready):
            r, c = tiles[k]
            down, along = pl.ds(r * 128, 128), pl.ds(c * 128, 128)
            middle = BETA * whole_a[pl.ds(k * 128, 128), :].astype(F32) + extra[down, along]
            middle = middle.astype(BF16)
            full[down, along] = middle
            if upper and r != c:
                full[along, down] = middle.T
        done = ready
    middle = full[...]
    share = block // 4
    for k in range(4):
        rows = pl.ds(pl.multiple_of(core * block + k * share, share), share)
        some = v_left[rows, :]
        new_root[rows, :] = (1.25 * some.astype(F32) - 0.25 * mm(some, middle)).astype(BF16)
        swap(new_root.at[rows], new_root.at[rows])
    swaps[0].wait_recv()
    own_g = owned(whole_g)
    has = owns[0] + owns[1]
    new_stats[...] = (BETA * has) * v_stats[...] + (1.0 - BETA) * mm_t(own_g, own_g)
    for move in z_moves:
        move.wait_recv()
    total = slots[0]
    for c in range(1, 2 * n_f):
        total = total + slots[c]
    total = jnp.sum(jnp.sum(total, axis=1, keepdims=True), axis=0, keepdims=True)
    scale = lax.rsqrt(total / entries + EPSILON)
    swaps[1].wait_recv()
    update[...] = (rounded[...].astype(F32) * scale).astype(BF16)
    for move in swaps[2:]:
        move.wait_recv()
    for s in streams:
        s.finish()
    for move in swaps + z_moves:
        move.wait_send()


def write_out(*refs):
    sources, targets, sems = refs[:3], refs[3:6], refs[6]
    pieces = sems.shape[1]
    moves = []
    for i, (src, dst) in enumerate(zip(sources, targets)):
        share = src.shape[0] // pieces
        for k in range(pieces):
            rows = pl.ds(k * share, share)
            moves.append(pltpu.make_async_copy(src.at[rows], dst.at[rows], sems.at[i, k]))
    for move in moves:
        move.start()
    for move in moves:
        move.wait()


def solution(mesh):
    n_dp, n_f = mesh.shape["dp"], mesh.shape["fsdp"]
    bits = n_dp.bit_length() - 1

    def local(grads, stats, left, right, owners):
        block = stats.shape[-1]
        rows = left.shape[0]
        count = block // 128
        upper = (len(tile_list(count, True)) * 128) % (16 * n_dp) == 0
        tiles = tile_list(count, upper)
        size = len(tiles) * 128
        pieces = 4 if size % (32 * n_dp) == 0 else 2
        parts = 4 if block % (32 * n_dp) == 0 else 2
        hbm = pl.BlockSpec(memory_space=pl.ANY)
        vmem = pl.BlockSpec(memory_space=pltpu.VMEM)
        dma = pltpu.SemaphoreType.DMA
        shapes = (
            jax.ShapeDtypeStruct((rows, block), BF16),
            jax.ShapeDtypeStruct((block, block), F32),
            jax.ShapeDtypeStruct((rows, block), BF16),
        )
        results = pl.pallas_call(
            functools.partial(kernel, n_dp, n_f, rows * block * n_f, tiles, upper),
            out_shape=shapes,
            in_specs=[pl.BlockSpec(memory_space=pltpu.HBM)] * 5,
            out_specs=(vmem, vmem, vmem),
            scratch_shapes=[
                pltpu.SMEM((2, n_f), jnp.int32),
                pltpu.VMEM((block, block), BF16),
                pltpu.VMEM((block, block), F32),
                pltpu.VMEM((rows, block), BF16),
                pltpu.VMEM((block, block), BF16),
                pltpu.VMEM((2 * size, 128), BF16),
                pltpu.VMEM((parts, 2 * block // parts, block), BF16),
                pltpu.VMEM((parts, 2 * block // parts, block), BF16),
                pltpu.VMEM((rows, block), BF16),
                pltpu.VMEM((pieces, 2 * size // pieces, 128), BF16),
                pltpu.VMEM((pieces, 2 * size // pieces, 128), BF16),
                pltpu.VMEM((size, 128), BF16),
                pltpu.VMEM((block, block), BF16),
                pltpu.VMEM((rows, block), BF16),
                pltpu.VMEM((block, block), F32),
                pltpu.VMEM((2 * n_f, 8, 128), F32),
                dma((5,)),
                dma((parts + pieces, bits)),
                dma((parts + pieces, bits)),
                dma((parts + pieces, bits)),
                dma((parts + pieces, bits)),
                dma((6,)),
                dma((6,)),
                dma((2 * n_f - 1,)),
                dma((2 * n_f - 1,)),
            ],
            compiler_params=pltpu.CompilerParams(
                collective_id=0, has_side_effects=True, vmem_limit_bytes=50 << 20
            ),
        )(owners.T, grads, stats, left, right)
        update, new_stats, new_root = pl.pallas_call(
            write_out,
            out_shape=shapes,
            in_specs=[hbm] * 3,
            out_specs=(hbm, hbm, hbm),
            scratch_shapes=[dma((3, 4))],
            compiler_params=pltpu.CompilerParams(vmem_limit_bytes=50 << 20),
        )(*results)
        return update, new_stats[None, None], new_root

    in_specs = (
        P("dp", None, "fsdp"),
        P("dp", "fsdp", None, None),
        P(None, "fsdp"),
        P(None, "fsdp"),
        P(),
    )
    out_specs = (P(None, "fsdp"), P("dp", "fsdp", None, None), P(None, "fsdp"))
    return jax.shard_map(local, mesh=mesh, in_specs=in_specs, out_specs=out_specs, check_vma=False)
```

```python
import functools

import jax
import jax.numpy as jnp
from jax import lax
from jax.experimental import pallas as pl
from jax.experimental.pallas import tpu as pltpu
from jax.sharding import PartitionSpec as P

BETA = 0.95
EPSILON = 1e-06
MESH = pl.DeviceIdType.MESH
F32 = jnp.float32
BF16 = jnp.bfloat16


def mm(a, b):
    return jnp.dot(a, b, preferred_element_type=F32)


def mm_t(a, b):
    return lax.dot_general(a, b, (((1,), (1,)), ((), ())), preferred_element_type=F32)


class Stream:
    def __init__(self, me, order, size, source, kept, near, away, recv, part, whole, base, sems):
        self.order, self.size, self.n = order, size, len(order)
        self.source, self.kept, self.near, self.away = source, kept, near, away
        self.recv, self.part, self.whole = recv, part, whole
        self.rs_send, self.rs_recv, self.ag_send, self.ag_recv = sems
        self.bit = [(me // (1 << b)) % 2 for b in order]
        self.peer = [me + (1 - 2 * v) * (1 << b) for v, b in zip(self.bit, order)]
        self.half = [size >> min(j, max(self.n - 2, 0)) for j in range(self.n)]
        self.at = [0] + [2 * size - (size >> (j - 1)) for j in range(1, self.n)]
        self.low = [base]
        for j in range(1, self.n - 1):
            self.low.append(self.low[-1] + self.bit[j] * self.half[j])
        self.pending = []

    def rows(self, start, size):
        return pl.ds(pl.multiple_of(start, 16), size)

    def copy(self, src, dst, send, recv, peer):
        move = pltpu.make_async_remote_copy(
            src_ref=src,
            dst_ref=dst,
            send_sem=send,
            recv_sem=recv,
            device_id={"dp": peer},
            device_id_type=MESH,
        )
        move.start()
        self.pending.append(move)
        return move

    def skip(self, j, v):
        return 0 if j == self.n - 1 else v * self.half[j]

    def start_sum(self, j):
        half = self.half[j]
        if j == 0:
            src = self.source.at[self.rows(self.away, half)]
        else:
            src = self.part.at[self.rows(self.at[j - 1] + self.skip(j, 1 - self.bit[j]), half)]
        self.move = self.copy(
            src,
            self.recv.at[pl.ds(self.at[j], half)],
            self.rs_send.at[j],
            self.rs_recv.at[j],
            self.peer[j],
        )

    def added(self, j, offset, size):
        if j == 0:
            mine = self.kept[self.rows(self.near + offset, size), :]
        else:
            near = self.at[j - 1] + self.skip(j, self.bit[j])
            mine = self.part[self.rows(near + offset, size), :]
        other = self.recv[self.rows(self.at[j] + offset, size), :]
        return (mine.astype(F32) + other.astype(F32)).astype(BF16)

    def end_sum(self, j):
        self.move.wait_recv()
        if j == self.n - 1:
            self.whole[self.rows(self.low[-1], self.half[j]), :] = self.added(j, 0, self.half[j])
            if j > 1:
                self.start_spread(j - 1)
            return
        if j == self.n - 2:
            self.part[self.rows(self.at[j], self.half[j]), :] = self.added(j, 0, self.half[j])
            self.start_sum(j + 1)
            return
        quarter = self.half[j + 1]
        v = self.bit[j + 1]
        self.part[self.rows(self.at[j] + (1 - v) * quarter, quarter), :] = self.added(
            j, (1 - v) * quarter, quarter
        )
        self.start_sum(j + 1)
        self.part[self.rows(self.at[j] + v * quarter, quarter), :] = self.added(
            j, v * quarter, quarter
        )

    def start_spread(self, j):
        here = self.whole.at[self.rows(self.low[j], self.half[j])]
        self.move = self.copy(here, here, self.ag_send.at[j], self.ag_recv.at[j], self.peer[j])

    def end_spread(self, j):
        self.move.wait_recv()
        if j > 1:
            self.start_spread(j - 1)

    def finish(self):
        for move in self.pending:
            move.wait_send()


def tile_list(count, upper):
    return [(r, c) for r in range(count) for c in range(r if upper else 0, count)]


def kernel(
    n_dp, n_f, entries, tiles, upper, owners_hbm, grads, stats, left, right,
    update, new_stats, new_root,
    owners, v_grads, v_stats, v_left, v_right, masked, recv_g, part_g, whole_g,
    recv_a, part_a, whole_a, full, rounded, extra,
    slots, local_sem, rs_send, rs_recv, ag_send, ag_recv, x_send, x_recv, z_send, z_recv,
):
    me = lax.axis_index("dp")
    col = lax.axis_index("fsdp")
    block = v_stats.shape[0]
    size = whole_a.shape[0]
    bits = n_dp.bit_length() - 1
    core = me % 2
    twin = me + 1 - 2 * core
    here = pl.ds(pl.multiple_of(core * block, block), block)

    loads = []
    for i, (src, dst) in enumerate(
        (
            (owners_hbm, owners), (stats.at[0, 0], v_stats), (left, v_left),
            (grads.at[0, here], v_grads), (right.at[here], v_right),
        )
    ):
        load = pltpu.make_async_copy(src, dst, local_sem.at[i])
        load.start()
        loads.append(load)

    partners = [{"dp": me + (1 - 2 * ((me // (1 << b)) % 2)) * (1 << b)} for b in range(bits)]
    others = []
    for o in range(1, n_f):
        others.append({"fsdp": lax.rem(col + o, n_f)})
        others.append({"dp": twin, "fsdp": lax.rem(col + o, n_f)})
    barrier = pltpu.get_barrier_semaphore()
    for device in partners + others:
        pl.semaphore_signal(barrier, inc=1, device_id=device, device_id_type=MESH)
    pl.semaphore_wait(barrier, len(partners) + len(others))
    others.append({"dp": twin})

    forward = list(range(bits))
    turned = [0] + forward[:0:-1]
    of_g, of_a = [], []
    for k in range(recv_g.shape[0]):
        order = forward if k % 2 == 0 else turned
        share = block // recv_g.shape[0]
        of_g.append(
            Stream(
                me, order, share, grads.at[0], v_grads,
                k * share, (1 - core) * block + k * share,
                recv_g.at[k], part_g.at[k], whole_g, core * block + k * share,
                (rs_send.at[k], rs_recv.at[k], ag_send.at[k], ag_recv.at[k]),
            )
        )
    for k in range(recv_a.shape[0]):
        order = forward if k % 2 == 0 else turned
        share = size // recv_a.shape[0]
        e = len(of_g) + k
        of_a.append(
            Stream(
                me, order, share, masked, masked,
                core * size + k * share, (1 - core) * size + k * share,
                recv_a.at[k], part_a.at[k], whole_a, k * share,
                (rs_send.at[e], rs_recv.at[e], ag_send.at[e], ag_recv.at[e]),
            )
        )
    streams = of_g + of_a
    swaps = []

    def swap(src, dst):
        move = pltpu.make_async_remote_copy(
            src_ref=src,
            dst_ref=dst,
            send_sem=x_send.at[len(swaps)],
            recv_sem=x_recv.at[len(swaps)],
            device_id={"dp": twin},
            device_id_type=MESH,
        )
        move.start()
        swaps.append(move)

    for s in of_g:
        s.start_sum(0)
    for load in loads[:3]:
        load.wait()
    owns = [jnp.where(owners[i, col] == me, 1.0, 0.0).astype(F32) for i in range(2)]

    def owned(ref):
        first = owns[0] * ref[pl.ds(0, block), :].astype(F32)
        return (first + owns[1] * ref[pl.ds(block, block), :].astype(F32)).astype(BF16)

    own_x = owned(v_left)
    own_q = mm(own_x, own_x).astype(BF16)
    loads[3].wait()
    for s in of_g[:2]:
        s.end_sum(0)
    own_t = mm(own_q, v_stats[...].astype(BF16)).astype(BF16)
    for s in of_g[2:]:
        s.end_sum(0)
    own_a = mm(own_t, own_q)
    for i in range(2):
        mine = (own_a * owns[i]).astype(BF16)
        for k, (r, c) in enumerate(tiles):
            masked[pl.ds(i * size + k * 128, 128), :] = mine[
                r * 128 : (r + 1) * 128, c * 128 : (c + 1) * 128
            ]
    for s in of_a:
        s.start_sum(0)
    x = v_left[here, :]
    q = mm(x, x).astype(BF16)
    for s in of_a:
        s.end_sum(0)
    for j in range(1, bits):
        for s in streams:
            s.end_sum(j)
    for j in range(bits - 2, 0, -1):
        for s in of_g:
            s.end_spread(j)
        if j > 1:
            for s in of_a:
                s.end_spread(j)
    swap(whole_g.at[here], whole_g.at[here])
    loads[4].wait()
    g = whole_g[here, :]
    raw = mm(mm(x, g).astype(BF16), v_right[...])
    rounded[here, :] = raw.astype(BF16)
    swap(rounded.at[here], rounded.at[here])
    power = jnp.sum((raw * raw).reshape(block // 8, 8, block), axis=0)
    squares = jnp.zeros((8, 128), F32)
    for c in range(0, block, 128):
        squares = squares + power[:, c : c + 128]
    slot = core * n_f + col
    slots[pl.ds(slot, 1), :, :] = squares[None]
    z_moves = []
    for i, device in enumerate(others):
        move = pltpu.make_async_remote_copy(
            src_ref=slots.at[slot],
            dst_ref=slots.at[slot],
            send_sem=z_send.at[i],
            recv_sem=z_recv.at[i],
            device_id=device,
            device_id_type=MESH,
        )
        move.start()
        z_moves.append(move)
    h = mm(q, g).astype(BF16)
    extra[...] = (1.0 - BETA) * mm_t(h, h)
    done = 0
    for i, s in enumerate(of_a):
        if bits > 2:
            s.end_spread(1)
        ready = (i + 1) * s.size // 128
        for k in range(done, ready):
            r, c = tiles[k]
            down, along = pl.ds(r * 128, 128), pl.ds(c * 128, 128)
            middle = BETA * whole_a[pl.ds(k * 128, 128), :].astype(F32) + extra[down, along]
            middle = middle.astype(BF16)
            full[down, along] = middle
            if upper and r != c:
                full[along, down] = middle.T
        done = ready
    middle = full[...]
    share = block // 4
    for k in range(4):
        rows = pl.ds(pl.multiple_of(core * block + k * share, share), share)
        some = v_left[rows, :]
        new_root[rows, :] = (1.25 * some.astype(F32) - 0.25 * mm(some, middle)).astype(BF16)
        swap(new_root.at[rows], new_root.at[rows])
    swaps[0].wait_recv()
    own_g = owned(whole_g)
    has = owns[0] + owns[1]
    new_stats[...] = (BETA * has) * v_stats[...] + (1.0 - BETA) * mm_t(own_g, own_g)
    for move in z_moves:
        move.wait_recv()
    total = slots[0]
    for c in range(1, 2 * n_f):
        total = total + slots[c]
    total = jnp.sum(jnp.sum(total, axis=1, keepdims=True), axis=0, keepdims=True)
    scale = lax.rsqrt(total / entries + EPSILON)
    swaps[1].wait_recv()
    update[...] = (rounded[...].astype(F32) * scale).astype(BF16)
    for move in swaps[2:]:
        move.wait_recv()
    for s in streams:
        s.finish()
    for move in swaps + z_moves:
        move.wait_send()


def write_out(*refs):
    sources, targets, sems = refs[:3], refs[3:6], refs[6]
    pieces = sems.shape[1]
    moves = []
    for i, (src, dst) in enumerate(zip(sources, targets)):
        share = src.shape[0] // pieces
        for k in range(pieces):
            rows = pl.ds(k * share, share)
            moves.append(pltpu.make_async_copy(src.at[rows], dst.at[rows], sems.at[i, k]))
    for move in moves:
        move.start()
    for move in moves:
        move.wait()


def solution(mesh):
    n_dp, n_f = mesh.shape["dp"], mesh.shape["fsdp"]
    bits = n_dp.bit_length() - 1

    def local(grads, stats, left, right, owners):
        block = stats.shape[-1]
        rows = left.shape[0]
        count = block // 128
        upper = (len(tile_list(count, True)) * 128) % (16 * n_dp) == 0
        tiles = tile_list(count, upper)
        size = len(tiles) * 128
        pieces = 2
        parts = 4 if block % (32 * n_dp) == 0 else 2
        hbm = pl.BlockSpec(memory_space=pl.ANY)
        vmem = pl.BlockSpec(memory_space=pltpu.VMEM)
        dma = pltpu.SemaphoreType.DMA
        shapes = (
            jax.ShapeDtypeStruct((rows, block), BF16),
            jax.ShapeDtypeStruct((block, block), F32),
            jax.ShapeDtypeStruct((rows, block), BF16),
        )
        results = pl.pallas_call(
            functools.partial(kernel, n_dp, n_f, rows * block * n_f, tiles, upper),
            out_shape=shapes,
            in_specs=[pl.BlockSpec(memory_space=pltpu.HBM)] * 5,
            out_specs=(vmem, vmem, vmem),
            scratch_shapes=[
                pltpu.SMEM((2, n_f), jnp.int32),
                pltpu.VMEM((block, block), BF16),
                pltpu.VMEM((block, block), F32),
                pltpu.VMEM((rows, block), BF16),
                pltpu.VMEM((block, block), BF16),
                pltpu.VMEM((2 * size, 128), BF16),
                pltpu.VMEM((parts, 2 * block // parts, block), BF16),
                pltpu.VMEM((parts, 2 * block // parts, block), BF16),
                pltpu.VMEM((rows, block), BF16),
                pltpu.VMEM((pieces, 2 * size // pieces, 128), BF16),
                pltpu.VMEM((pieces, 2 * size // pieces, 128), BF16),
                pltpu.VMEM((size, 128), BF16),
                pltpu.VMEM((block, block), BF16),
                pltpu.VMEM((rows, block), BF16),
                pltpu.VMEM((block, block), F32),
                pltpu.VMEM((2 * n_f, 8, 128), F32),
                dma((5,)),
                dma((parts + pieces, bits)),
                dma((parts + pieces, bits)),
                dma((parts + pieces, bits)),
                dma((parts + pieces, bits)),
                dma((6,)),
                dma((6,)),
                dma((2 * n_f - 1,)),
                dma((2 * n_f - 1,)),
            ],
            compiler_params=pltpu.CompilerParams(
                collective_id=0, has_side_effects=True, vmem_limit_bytes=50 << 20
            ),
        )(owners.T, grads, stats, left, right)
        update, new_stats, new_root = pl.pallas_call(
            write_out,
            out_shape=shapes,
            in_specs=[hbm] * 3,
            out_specs=(hbm, hbm, hbm),
            scratch_shapes=[dma((3, 4))],
            compiler_params=pltpu.CompilerParams(vmem_limit_bytes=50 << 20),
        )(*results)
        return update, new_stats[None, None], new_root

    in_specs = (
        P("dp", None, "fsdp"),
        P("dp", "fsdp", None, None),
        P(None, "fsdp"),
        P(None, "fsdp"),
        P(),
    )
    out_specs = (P(None, "fsdp"), P("dp", "fsdp", None, None), P(None, "fsdp"))
    return jax.shard_map(local, mesh=mesh, in_specs=in_specs, out_specs=out_specs, check_vma=False)
```
